32 devices in a mesh: row: 2 (over core), sec: 4 (over y, x), span: 4 (over z).
Axes of the slice: x: 2, y: 2, z: 4, core: 2. Of those that a mesh axis runs over, the one named last changes fastest.
Arguments:
- state: float32 [2, 9, 7, 4, 16, 512], P('row', None, None, None, 'span', 'sec'), may hold values from -6 to 6
- viscosity: float32 [2, 4, 16, 512], P('row', None, 'span', 'sec'), may hold values from 0.1 to 1
- jacobian: float32 [2, 7, 7], P('row'), may hold values from -2 to 2
- frequency: float32 [2], P('row'), may hold values from 0.5 to 2
- offsets: int32 [9], replicated, may hold values from 0 to 511
Outputs:
- updated: float32 [2, 9, 7, 4, 16, 512], P('row', None, None, None, 'span', 'sec')
The draws below stay inside these ranges and needn't reach their ends.
All inputs are finite; a program needn't handle non-finite values.
Results may differ from the reference program's by a relative error of at most 0.0001.
Values sent between devices are 32-bit elements; how exact they have to be, the bound alone decides.
No kernel may reach another device: no remote copies, remote signals or barrier semaphores. Data moves between devices by JAX's collectives and lax.ppermute only.
A program may use at most 192 MiB of HBM per device.

```python
import math
import jax
import jax.numpy as jnp
from jax import lax

INSTANCES = 9
FIELDS = 7
AXIAL = 4
ROWS = 2
NS = 16
NT = 512


def touch_ends(drawn, stream_key, low, high):
    place = [jax.random.randint(jax.random.fold_in(stream_key, axis), (), 0, length) for axis, length in enumerate(drawn.shape)]
    widest = drawn.shape.index(max(drawn.shape))
    next_to = place[:widest] + [(place[widest] + 1) % drawn.shape[widest]] + place[widest + 1:]
    return drawn.at[tuple(place)].set(low).at[tuple(next_to)].set(high)


def block_scale(stream_key, dims, cuts, least, top_value):
    def one(dim, blocks):
        heights = jax.random.uniform(jax.random.fold_in(jax.random.fold_in(stream_key, 6), dim), (blocks,), jnp.float32, least / len(cuts), top_value / len(cuts))
        return jnp.repeat(jnp.exp(heights), dims[dim] // blocks).reshape((-1,) + (1,) * (len(dims) - dim - 1))

    loudness = one(*cuts[0])
    for cut in cuts[1:]:
        loudness = loudness * one(*cut)
    return loudness


def noise(stream_key, dims, spread, most, shards=(), dtype=jnp.bfloat16):
    gain = block_scale(stream_key, dims, shards, -0.22, 0.18) if shards else 1.0
    values = jax.random.normal(stream_key, dims, jnp.float32) * spread * gain
    return jnp.minimum(jnp.maximum(values, -most), most).astype(dtype)


def setup_inputs(seed: int = 0) -> dict:
    arg_keys = jax.random.split(jax.random.key(seed), 6)
    return {
        "state": noise(arg_keys[0], (ROWS, INSTANCES, FIELDS, AXIAL, NS, NT), 1.0, 6.0, ((0, 2), (4, 4), (5, 4)), jnp.float32),
        "viscosity": jnp.clip(jnp.exp(math.log(1.0) - 2.3025851 * jax.random.uniform(arg_keys[1], (ROWS, AXIAL, NS, NT), jnp.float32) ** block_scale(arg_keys[1], (ROWS, AXIAL, NS, NT), ((0, 2), (2, 4), (3, 4)), -0.2, 0.2)), 0.1, 1.0),
        "jacobian": noise(arg_keys[2], (ROWS, FIELDS, FIELDS), FIELDS ** -0.5, 2.0, ((0, 2),), jnp.float32),
        "frequency": jnp.clip(jnp.exp(math.log(2.0) - 1.3862944 * jax.random.uniform(arg_keys[3], (ROWS,), jnp.float32) ** block_scale(arg_keys[3], (ROWS,), ((0, 2),), -0.2, 0.2)), 0.5, 2.0),
        "offsets": touch_ends(jax.random.randint(arg_keys[4], (INSTANCES,), 0, NT), jax.random.fold_in(arg_keys[4], 1), 0, NT - 1).astype(jnp.int32),
    }


def spectral_matrix(count):
    index = jnp.arange(count)
    offset = index[:, None] - index[None, :]
    parity = jnp.where(jnp.abs(offset) % 2 == 0, 1.0, -1.0).astype(jnp.float32)
    angle = (math.pi / count) * offset.astype(jnp.float32)
    safe_sin = jnp.where(offset == 0, jnp.float32(1.0), jnp.sin(angle))
    return jnp.where(offset == 0, jnp.float32(0.0), 0.5 * parity / safe_sin).astype(jnp.float32)


def reference(state, viscosity, jacobian, frequency, offsets):
    deriv = spectral_matrix(INSTANCES)
    collected_outputs = []
    for which in range(2):
        flow_field_values = state[which]
        other = state[1 - which][:, :, -1]
        if which == 0:
            shift = offsets
        else:
            shift = (NT - offsets) % NT
        ghost = jax.vmap(lambda block, amount: jnp.roll(block, amount, axis=-1))(other, shift)
        plus_theta = jnp.roll(flow_field_values, -1, axis=-1)
        minus_theta = jnp.roll(flow_field_values, 1, axis=-1)
        padded = jnp.pad(flow_field_values, ((0, 0), (0, 0), (0, 0), (1, 1), (0, 0)))
        upper_spanwise_neighbour = padded[:, :, :, 2:]
        lower_spanwise_neighbour = padded[:, :, :, :-2]
        plus_axial = jnp.concatenate([flow_field_values[:, :, 1:], ghost[:, :, None]], axis=2)
        minus_axial = jnp.concatenate([jnp.zeros_like(flow_field_values[:, :, :1]), flow_field_values[:, :, :-1]], axis=2)
        timeterm = jnp.einsum("tu,ufasc->tfasc", deriv, flow_field_values, precision=lax.Precision.HIGHEST)
        convect = jnp.einsum("fg,tgasc->tfasc", jacobian[which], plus_theta - minus_theta, precision=lax.Precision.HIGHEST)
        coeff = viscosity[which]
        residual = (-frequency[which] * timeterm - 0.5 * convect
                    + coeff * (plus_theta + minus_theta - 2.0 * flow_field_values)
                    + coeff * (upper_spanwise_neighbour + lower_spanwise_neighbour - 2.0 * flow_field_values)
                    + (plus_axial + minus_axial - 2.0 * flow_field_values))
        collected_outputs.append(flow_field_values + 0.1 * residual)
    return jnp.stack(collected_outputs)
```

```python
import math

import jax
import jax.numpy as jnp
from jax import lax
from jax.experimental import pallas as pl
from jax.experimental.pallas import tpu as pltpu
from jax.sharding import PartitionSpec as P

VMEM = pl.BlockSpec(memory_space=pltpu.VMEM)
SMEM = pl.BlockSpec(memory_space=pltpu.SMEM)


def pairs(count, first, periodic):
    route = []
    for low in range(first, count, 2):
        high = low + 1
        if high < count or periodic:
            high %= count
            route += [(low, high), (high, low)]
    return route


def crossed(count, distance):
    return [
        (row * count + here, (1 - row) * count + (here ^ distance))
        for row in range(2)
        for here in range(count)
    ]


def pack_kernel(tiles, state_ref, strip_ref, even_ref, odd_ref, edge_ref):
    parity = lax.axis_index("span") % 2
    lane = lax.broadcasted_iota(jnp.int32, (16, 128), 1)
    low = state_ref[pl.ds(0, 4 * tiles, stride=4), :]
    high = state_ref[pl.ds(3, 4 * tiles, stride=4), :]
    even_ref[...] = jnp.where(parity == 0, high, low)
    odd_ref[...] = jnp.where(parity == 0, low, high)

    def step(i, edge):
        block = state_ref[pl.ds(pl.multiple_of(i * 16, 16), 16), :]
        strip_ref[i] = block[12:]
        turned = pltpu.roll(block, 2 * i + 1, 1)
        return jnp.where(lane // 2 == i, turned, edge)

    edge_ref[...] = lax.fori_loop(0, tiles, step, jnp.zeros((16, 128), jnp.float32), unroll=7)


def update_kernel(
    times,
    fields,
    slots,
    state_ref,
    coeff_ref,
    jac_ref,
    omega_ref,
    offset_ref,
    even_ref,
    odd_ref,
    edge_a_ref,
    edge_b_ref,
    *rest,
):
    source_refs, out_ref = rest[:-1], rest[-1]
    sectors = lax.axis_size("sec")
    row = lax.axis_index("row")
    sec = lax.axis_index("sec")
    span_parity = lax.axis_index("span") % 2
    sec_parity = sec % 2
    lane = lax.broadcasted_iota(jnp.int32, (8, 128), 1)
    sub = lax.broadcasted_iota(jnp.int32, (8, 128), 0)
    lower = sub < 4
    bottom = sub % 4 == 0
    top = sub % 4 == 3
    lane4 = lax.broadcasted_iota(jnp.int32, (4, 128), 1)

    edge_a, edge_b = edge_a_ref[...], edge_b_ref[...]
    plus_edge = jnp.where(sec_parity == 0, edge_a, edge_b)
    minus_edge = jnp.where(sec_parity == 0, edge_b, edge_a)
    wide_lane = lax.broadcasted_iota(jnp.int32, (16, 128), 1)
    halo = jnp.where(
        wide_lane % 2 == 0, pltpu.roll(plus_edge, 127, 1), pltpu.roll(minus_edge, 1, 1)
    )
    coeff = [0.1 * coeff_ref[0:8, :], 0.1 * coeff_ref[8:16, :]]
    own = [0.8 - 4.0 * c for c in coeff]
    rate = -0.1 * omega_ref[0]
    weight = [0.0]
    weight += [0.5 * (-1.0) ** m / math.sin(math.pi * m / times) for m in range(1, times)]

    def pick(slot, index):
        if len(source_refs) == 1:
            return source_refs[0][slot, index]
        value = source_refs[0][index]
        for other in range(1, slots):
            value = jnp.where(slot == other, source_refs[other][index], value)
        return value

    def step(t, _):
        offset = offset_ref[t]
        total = sectors * 128
        shift = jnp.where(row == 0, offset, lax.rem(total - offset, total))
        whole, part = shift // 128, shift % 128
        near = lax.rem(sec - whole + sectors, sectors)
        far = lax.rem(sec - whole - 1 + sectors + sectors, sectors)
        if len(source_refs) > 1:
            near, far = near ^ sec, far ^ sec

        def load(u, f, h):
            start = pl.multiple_of((u * fields + f) * 16 + 8 * h, 8)
            return state_ref[pl.ds(start, 8), :]

        centre = [[load(t, f, h) for h in range(2)] for f in range(fields)]
        difference, result = [], []
        for f in range(fields):
            index = t * fields + f
            turned = pltpu.roll(halo, 127 - 2 * index, 1)
            ghost = pick(near, index)
            ghost_far = pick(far, index)
            ghost = pltpu.roll(jnp.where(lane4 >= 128 - part, ghost_far, ghost), part, 1)
            ghost = jnp.concatenate([ghost, ghost], axis=0)
            v0, v1 = centre[f]
            r0, r1 = pltpu.roll(v0, 4, 0), pltpu.roll(v1, 4, 0)
            middle = jnp.where(lower, r0, r1)
            axial = [
                middle + jnp.where(lower, 0.0, r0),
                jnp.where(lower, r1, ghost) + middle,
            ]
            differences, results = [], []
            for h in range(2):
                v = centre[f][h]
                edge = turned[8 * h : 8 * h + 8]
                plus = jnp.where(lane == 127, edge, pltpu.roll(v, 127, 1))
                minus = jnp.where(lane == 0, edge, pltpu.roll(v, 1, 1))
                start = 4 * index + 2 * h
                even = jnp.where(
                    lower, even_ref[pl.ds(start, 1), :], even_ref[pl.ds(start + 1, 1), :]
                )
                odd = jnp.where(
                    lower, odd_ref[pl.ds(start, 1), :], odd_ref[pl.ds(start + 1, 1), :]
                )
                up_halo = jnp.where(span_parity == 0, even, odd)
                down_halo = jnp.where(span_parity == 0, odd, even)
                up = jnp.where(top, up_halo, pltpu.roll(v, 7, 0))
                down = jnp.where(bottom, down_halo, pltpu.roll(v, 1, 0))
                differences.append(plus - minus)
                value = own[h] * v + coeff[h] * ((plus + minus) + (up + down)) + 0.1 * axial[h]
                spectral = jnp.zeros_like(v)
                for m in range(1, times // 2 + 1):
                    before = load(lax.rem(t + times - m, times), f, h)
                    after = load(lax.rem(t + m, times), f, h)
                    spectral = spectral + weight[m] * (before - after)
                results.append(value + rate * spectral)
            difference.append(differences)
            result.append(results)
        for f in range(fields):
            for h in range(2):
                value = result[f][h]
                for g in range(fields):
                    value = value + (-0.05 * jac_ref[f, g]) * difference[g][h]
                start = pl.multiple_of((t * fields + f) * 16 + 8 * h, 8)
                out_ref[pl.ds(start, 8), :] = value
        return 0

    lax.fori_loop(0, times, step, 0)


def on_device(state, viscosity, jacobian, frequency, offsets):
    _, times, fields, axial, spans, cells = state.shape
    tiles = times * fields
    sectors, slabs = lax.axis_size("sec"), lax.axis_size("span")
    flat = state.reshape(tiles * 16, cells)
    strip, even, odd, edge = pl.pallas_call(
        lambda *refs: pack_kernel(tiles, *refs),
        out_shape=[
            jax.ShapeDtypeStruct((tiles, 4, cells), jnp.float32),
            jax.ShapeDtypeStruct((tiles * 4, cells), jnp.float32),
            jax.ShapeDtypeStruct((tiles * 4, cells), jnp.float32),
            jax.ShapeDtypeStruct((16, cells), jnp.float32),
        ],
        in_specs=[VMEM],
        out_specs=[VMEM] * 4,
        name="pack",
    )(flat)
    odd = lax.ppermute(odd, "span", pairs(slabs, 1, False))
    even = lax.ppermute(even, "span", pairs(slabs, 0, False))
    edge_b = lax.ppermute(edge, "sec", pairs(sectors, 1, True))
    edge_a = lax.ppermute(edge, "sec", pairs(sectors, 0, True))
    swapped = lax.ppermute(strip, "row", [(0, 1), (1, 0)])
    if sectors == 4:
        sources = [swapped] + [
            lax.ppermute(strip, ("row", "sec"), crossed(sectors, distance)) for distance in (1, 2, 3)
        ]
    else:
        sources = [lax.all_gather(swapped, "sec")]
    out = pl.pallas_call(
        lambda *refs: update_kernel(times, fields, sectors, *refs),
        out_shape=jax.ShapeDtypeStruct(flat.shape, jnp.float32),
        in_specs=[VMEM, VMEM, SMEM, SMEM, SMEM] + [VMEM] * (4 + len(sources)),
        out_specs=VMEM,
        compiler_params=pltpu.CompilerParams(vmem_limit_bytes=32 * 1024 * 1024),
        name="update",
    )(
        flat,
        viscosity.reshape(16, cells),
        jacobian[0],
        frequency,
        offsets,
        even,
        odd,
        edge_a,
        edge_b,
        *sources,
    )
    return out.reshape(state.shape)


def solution(mesh):
    return jax.shard_map(
        on_device,
        mesh=mesh,
        in_specs=(
            P("row", None, None, None, "span", "sec"),
            P("row", None, "span", "sec"),
            P("row", None, None),
            P("row"),
            P(),
        ),
        out_specs=P("row", None, None, None, "span", "sec"),
        check_vma=False,
    )
```

```python
import math

import jax
import jax.numpy as jnp
from jax import lax
from jax.experimental import pallas as pl
from jax.experimental.pallas import tpu as pltpu
from jax.sharding import PartitionSpec as P

VMEM = pl.BlockSpec(memory_space=pltpu.VMEM)
SMEM = pl.BlockSpec(memory_space=pltpu.SMEM)
ANY = pl.BlockSpec(memory_space=pl.ANY)
LIMIT = pltpu.CompilerParams(vmem_limit_bytes=32 * 1024 * 1024)


def sector_pairs(count, first):
    return [
        pair
        for low in range(first, count, 2)
        for pair in ((low, (low + 1) % count), ((low + 1) % count, low))
    ]


def slab_pairs(count, first):
    route = []
    for row in range(2):
        for here in range(count):
            there = here ^ 1 if first == 0 else ((here - 1) ^ 1) + 1
            if 0 <= there < count:
                route.append((row * count + here, row * count + there))
            else:
                route.append((row * count + here, (1 - row) * count + here))
    return route


def collect_kernel(tiles, source_ref, state_ref, strip_ref, even_ref, odd_ref, sem):
    copy = pltpu.make_async_copy(source_ref, state_ref, sem)
    copy.start()
    slab, slabs = lax.axis_index("span"), lax.axis_size("span")
    parity = lax.rem(slab, 2)
    paired_even = (slab ^ 1) < slabs
    paired_odd = jnp.logical_and(slab > 0, ((slab - 1) ^ 1) + 1 < slabs)
    copy.wait()
    low = state_ref[pl.ds(0, 4 * tiles, stride=4), :]
    high = state_ref[pl.ds(3, 4 * tiles, stride=4), :]
    even_ref[...] = jnp.where(paired_even, jnp.where(parity == 0, high, low), 0.0)
    odd_ref[...] = jnp.where(paired_odd, jnp.where(parity == 0, low, high), 0.0)

    def step(i, _):
        strip_ref[i] = state_ref[pl.ds(i * 16 + 12, 4), :]
        return 0

    lax.fori_loop(0, tiles, step, 0, unroll=9)


def edge_kernel(tiles, state_ref, edge_ref):
    lane = lax.broadcasted_iota(jnp.int32, (16, 128), 1)

    def step(i, edge):
        block = state_ref[pl.ds(pl.multiple_of(i * 16, 16), 16), :]
        return jnp.where(lane // 2 == i, pltpu.roll(block, 2 * i + 1, 1), edge)

    edge = lax.fori_loop(0, tiles, step, jnp.zeros((16, 128), jnp.float32), unroll=7)
    for a in range(4):
        edge_ref[a] = edge[4 * a : 4 * a + 4]


def inner_kernel(
    times,
    fields,
    state_ref,
    coeff_ref,
    jac_ref,
    omega_ref,
    offset_ref,
    _,
    partial_ref,
    mix_ref,
    place_ref,
):
    sectors = lax.axis_size("sec")
    row, sec = lax.axis_index("row"), lax.axis_index("sec")
    lane = lax.broadcasted_iota(jnp.int32, (8, 128), 1)
    sub = lax.broadcasted_iota(jnp.int32, (8, 128), 0)
    lower = sub < 4
    bottom = sub % 4 == 0
    top = sub % 4 == 3
    coeff = [0.1 * coeff_ref[0:8, :], 0.1 * coeff_ref[8:16, :]]
    own = [0.8 - 4.0 * c for c in coeff]
    rate = -0.1 * omega_ref[0]
    weight = [0.0]
    weight += [0.5 * (-1.0) ** m / math.sin(math.pi * m / times) for m in range(1, times)]

    field = (lane // 2) % fields
    sign = jnp.where(lane % 2 == 0, -0.05, 0.05)
    for distance in range(1 - fields, fields):
        mix = jnp.zeros((8, 128), jnp.float32)
        for f in range(max(0, distance), min(fields, fields + distance)):
            mix = jnp.where(field == f, jac_ref[f, f - distance], mix)
        mix_ref[fields - 1 + distance] = sign * mix

    def step(t, _):
        offset = offset_ref[t]
        total = sectors * 128
        shift = jnp.where(row == 0, offset, lax.rem(total - offset, total))
        whole = shift // 128
        near = lax.rem(sec - whole + sectors, sectors)
        far = lax.rem(sec - whole - 1 + 2 * sectors, sectors)
        if sectors == 4:
            near, far = near ^ sec, far ^ sec
        place_ref[3 * t] = near
        place_ref[3 * t + 1] = far
        place_ref[3 * t + 2] = shift - 128 * whole

        def load(u, f, h):
            start = pl.multiple_of((u * fields + f) * 16 + 8 * h, 8)
            return state_ref[pl.ds(start, 8), :]

        difference, result = [], []
        for f in range(fields):
            v0, v1 = load(t, f, 0), load(t, f, 1)
            r0, r1 = pltpu.roll(v0, 4, 0), pltpu.roll(v1, 4, 0)
            middle = jnp.where(lower, r0, r1)
            axial = [middle + jnp.where(lower, 0.0, r0), jnp.where(lower, r1, 0.0) + middle]
            differences, results = [], []
            for h, v in enumerate((v0, v1)):
                plus = jnp.where(lane == 127, 0.0, pltpu.roll(v, 127, 1))
                minus = jnp.where(lane == 0, 0.0, pltpu.roll(v, 1, 1))
                up = jnp.where(top, 0.0, pltpu.roll(v, 7, 0))
                down = jnp.where(bottom, 0.0, pltpu.roll(v, 1, 0))
                differences.append(plus - minus)
                value = own[h] * v + coeff[h] * ((plus + minus) + (up + down)) + 0.1 * axial[h]
                spectral = jnp.zeros_like(v)
                for m in range(1, times // 2 + 1):
                    before = load(lax.rem(t + times - m, times), f, h)
                    after = load(lax.rem(t + m, times), f, h)
                    spectral = spectral + weight[m] * (before - after)
                results.append(value + rate * spectral)
            difference.append(differences)
            result.append(results)
        for f in range(fields):
            for h in range(2):
                value = result[f][h]
                for g in range(fields):
                    value = value + (-0.05 * jac_ref[f, g]) * difference[g][h]
                start = pl.multiple_of((t * fields + f) * 16 + 8 * h, 8)
                partial_ref[pl.ds(start, 8), :] = value
        return 0

    lax.fori_loop(0, times, step, 0)


def outer_kernel(
    times,
    fields,
    slots,
    partial_ref,
    mix_ref,
    place_ref,
    coeff_ref,
    even_ref,
    odd_ref,
    edge_a_ref,
    edge_b_ref,
    *rest,
):
    source_refs, (out_ref, span_ref, total_ref, sems) = rest[:-4], rest[-4:]
    tiles = times * fields
    sec_parity = lax.rem(lax.axis_index("sec"), 2)
    span_parity = lax.rem(lax.axis_index("span"), 2)
    lane = lax.broadcasted_iota(jnp.int32, (8, 128), 1)
    sub = lax.broadcasted_iota(jnp.int32, (8, 128), 0)
    lane4 = lax.broadcasted_iota(jnp.int32, (4, 128), 1)
    border = jnp.logical_or(sub % 4 == 0, sub % 4 == 3)
    lower = sub < 4
    outside = jnp.logical_or(lane == 0, lane == 127)
    sides = lane % 2 == 0

    even, odd = even_ref[...], odd_ref[...]
    coeff_low = 0.1 * coeff_ref[pl.ds(0, 4, stride=4), :]
    coeff_high = 0.1 * coeff_ref[pl.ds(3, 4, stride=4), :]
    up = jnp.where(span_parity == 0, even, odd).reshape(tiles, 4, 128) * coeff_high[None]
    down = jnp.where(span_parity == 0, odd, even).reshape(tiles, 4, 128) * coeff_low[None]
    span_ref[pl.ds(3, 4 * tiles, stride=4), :] = up.reshape(4 * tiles, 128)
    span_ref[pl.ds(0, 4 * tiles, stride=4), :] = down.reshape(4 * tiles, 128)

    edges = []
    for h in range(2):
        edge_a = jnp.concatenate([edge_a_ref[tiles_at] for tiles_at in (2 * h, 2 * h + 1)], axis=0)
        edge_b = jnp.concatenate([edge_b_ref[tiles_at] for tiles_at in (2 * h, 2 * h + 1)], axis=0)
        plus_edge = jnp.where(sec_parity == 0, edge_a, edge_b)
        minus_edge = jnp.where(sec_parity == 0, edge_b, edge_a)
        halo = jnp.where(sides, pltpu.roll(plus_edge, 127, 1), pltpu.roll(minus_edge, 1, 1))
        coeff = 0.1 * coeff_ref[8 * h : 8 * h + 8, :]
        term = jnp.where(sides, coeff[:, 127:128], coeff[:, 0:1]) * halo
        for distance in range(1 - fields, fields):
            term = term + mix_ref[fields - 1 + distance] * pltpu.roll(halo, (2 * distance) % 128, 1)
        edges.append(term)

    def pick(slot, index):
        if len(source_refs) == 1:
            return source_refs[0][slot, index]
        value = source_refs[0][index]
        for other in range(1, slots):
            value = jnp.where(slot == other, source_refs[other][index], value)
        return value

    def piece(t):
        rows = pl.ds(pl.multiple_of(t * fields * 16, 16), fields * 16)
        return pltpu.make_async_copy(total_ref.at[rows, :], out_ref.at[rows, :], sems.at[t])

    def step(t, _):
        near, far, part = place_ref[3 * t], place_ref[3 * t + 1], place_ref[3 * t + 2]
        for f in range(fields):
            index = t * fields + f
            ghost = jnp.where(lane4 >= 128 - part, pick(far, index), pick(near, index))
            ghost = pltpu.roll(ghost, part, 1)
            ghost = jnp.concatenate([ghost, ghost], axis=0)
            for h in range(2):
                rows = pl.ds(pl.multiple_of(index * 16 + 8 * h, 8), 8)
                value = partial_ref[rows, :] + jnp.where(border, span_ref[rows, :], 0.0)
                value = value + jnp.where(outside, pltpu.roll(edges[h], 127 - 2 * index, 1), 0.0)
                if h == 1:
                    value = value + jnp.where(lower, 0.0, 0.1 * ghost)
                total_ref[rows, :] = value
        piece(t).start()
        return 0

    lax.fori_loop(0, times, step, 0)
    for t in range(times):
        piece(t).wait()


def on_device(state, viscosity, jacobian, frequency, offsets):
    _, times, fields, axial, spans, cells = state.shape
    tiles = times * fields
    sectors, slabs = lax.axis_size("sec"), lax.axis_size("span")
    flat = state.reshape(tiles * 16, cells)
    coeff = viscosity.reshape(16, cells)
    f32 = jnp.float32
    local, strip, even, odd = pl.pallas_call(
        lambda *refs: collect_kernel(tiles, *refs),
        out_shape=[
            pltpu.VMEM((tiles * 16, cells), f32),
            pltpu.VMEM((tiles, 4, cells), f32),
            pltpu.VMEM((tiles * 4, cells), f32),
            pltpu.VMEM((tiles * 4, cells), f32),
        ],
        in_specs=[ANY],
        out_specs=[VMEM] * 4,
        scratch_shapes=[pltpu.SemaphoreType.DMA],
        compiler_params=LIMIT,
        name="collect",
    )(flat)
    swapped = lax.ppermute(strip, "row", [(0, 1), (1, 0)])
    edge = pl.pallas_call(
        lambda *refs: edge_kernel(tiles, *refs),
        out_shape=pltpu.VMEM((4, 4, cells), f32),
        in_specs=[VMEM],
        out_specs=VMEM,
        compiler_params=LIMIT,
        name="edges",
    )(local)
    packed = jnp.concatenate([swapped, edge], axis=0)
    even = lax.ppermute(even, ("row", "span"), slab_pairs(slabs, 0))
    odd = lax.ppermute(odd, ("row", "span"), slab_pairs(slabs, 1))
    if sectors == 4:
        near = [
            lax.ppermute(packed, "sec", [(k, k ^ distance) for k in range(sectors)])
            for distance in (1, 2, 3)
        ]
        sources = [swapped] + near
        edge_a = edge_b = None
        edge_a, edge_b = near[0][tiles:], near[2][tiles:]
    else:
        sources = [lax.all_gather(swapped, "sec")]
        edge_a = lax.ppermute(edge, "sec", sector_pairs(sectors, 0))
        edge_b = lax.ppermute(edge, "sec", sector_pairs(sectors, 1))
    partial, mix, place = pl.pallas_call(
        lambda *refs: inner_kernel(times, fields, *refs),
        out_shape=[
            pltpu.VMEM((tiles * 16, cells), f32),
            pltpu.VMEM((2 * fields - 1, 8, cells), f32),
            pltpu.SMEM((3 * times,), jnp.int32),
        ],
        in_specs=[VMEM, VMEM, SMEM, SMEM, SMEM, ANY],
        out_specs=[VMEM, VMEM, SMEM],
        compiler_params=LIMIT,
        cost_estimate=pl.CostEstimate(
            flops=tiles * 16 * cells * 50, bytes_accessed=tiles * 16 * cells * 8, transcendentals=0
        ),
        name="inner",
    )(local, coeff, jacobian[0], frequency, offsets, packed)
    out = pl.pallas_call(
        lambda *refs: outer_kernel(times, fields, sectors, *refs),
        out_shape=jax.ShapeDtypeStruct(flat.shape, f32),
        in_specs=[VMEM, VMEM, SMEM] + [VMEM] * (5 + len(sources)),
        out_specs=ANY,
        scratch_shapes=[
            pltpu.VMEM((tiles * 16, cells), f32),
            pltpu.VMEM((tiles * 16, cells), f32),
            pltpu.SemaphoreType.DMA((times,)),
        ],
        compiler_params=LIMIT,
        name="outer",
    )(partial, mix, place, coeff, even, odd, edge_a, edge_b, *sources)
    return out.reshape(state.shape)


def solution(mesh):
    return jax.shard_map(
        on_device,
        mesh=mesh,
        in_specs=(
            P("row", None, None, None, "span", "sec"),
            P("row", None, "span", "sec"),
            P("row", None, None),
            P("row"),
            P(),
        ),
        out_specs=P("row", None, None, None, "span", "sec"),
        check_vma=False,
    )
```

```python
import math

import jax
import jax.numpy as jnp
from jax import lax
from jax.experimental import pallas as pl
from jax.experimental.pallas import tpu as pltpu
from jax.sharding import PartitionSpec as P

VMEM = pl.BlockSpec(memory_space=pltpu.VMEM)
SMEM = pl.BlockSpec(memory_space=pltpu.SMEM)
ANY = pl.BlockSpec(memory_space=pl.ANY)
LIMIT = pltpu.CompilerParams(vmem_limit_bytes=32 * 1024 * 1024)


def sector_pairs(count, first):
    return [
        pair
        for low in range(first, count, 2)
        for pair in ((low, (low + 1) % count), ((low + 1) % count, low))
    ]


def slab_pairs(count, first):
    route = []
    for row in range(2):
        for here in range(count):
            there = here ^ 1 if first == 0 else ((here - 1) ^ 1) + 1
            if 0 <= there < count:
                route.append((row * count + here, row * count + there))
            else:
                route.append((row * count + here, (1 - row) * count + here))
    return route


def collect_kernel(
    times,
    fields,
    source_ref,
    offset_source_ref,
    state_ref,
    edge_ref,
    even_ref,
    odd_ref,
    place_ref,
    offset_ref,
    sems,
    offset_sem,
):
    block_rows = fields * 16
    plan = pltpu.make_async_copy(offset_source_ref, offset_ref, offset_sem)

    def piece(t):
        rows = pl.ds(t * block_rows, block_rows)
        return pltpu.make_async_copy(source_ref.at[rows, :], state_ref.at[rows, :], sems.at[t])

    for t in range(times):
        piece(t).start()
    plan.start()
    lane = lax.broadcasted_iota(jnp.int32, (16, 128), 1)
    edge = jnp.zeros((16, 128), jnp.float32)
    for t in range(times):
        piece(t).wait()
        for f in range(fields):
            i = t * fields + f
            block = state_ref[pl.ds(16 * i, 16), :]
            here = jnp.logical_or(lane == 2 * i, lane == 2 * i + 1)
            edge = jnp.where(here, pltpu.roll(block, 2 * i + 1, 1), edge)
    for a in range(4):
        edge_ref[a] = edge[4 * a : 4 * a + 4]

    slab, slabs = lax.axis_index("span"), lax.axis_size("span")
    parity = lax.rem(slab, 2)
    paired_even = (slab ^ 1) < slabs
    paired_odd = jnp.logical_and(slab > 0, ((slab - 1) ^ 1) + 1 < slabs)
    low = state_ref[pl.ds(0, 4 * times * fields, stride=4), :]
    high = state_ref[pl.ds(3, 4 * times * fields, stride=4), :]
    even_ref[...] = jnp.where(paired_even, jnp.where(parity == 0, high, low), 0.0)
    odd_ref[...] = jnp.where(paired_odd, jnp.where(parity == 0, low, high), 0.0)

    plan.wait()
    sectors = lax.axis_size("sec")
    row, sec = lax.axis_index("row"), lax.axis_index("sec")
    total = sectors * 128
    for t in range(times):
        offset = offset_ref[t]
        shift = jnp.where(row == 0, offset, lax.rem(total - offset, total))
        whole = shift // 128
        near = lax.rem(sec - whole + sectors, sectors)
        far = lax.rem(sec - whole - 1 + 2 * sectors, sectors)
        if sectors == 4:
            near, far = near ^ sec, far ^ sec
        place_ref[3 * t] = near
        place_ref[3 * t + 1] = far
        place_ref[3 * t + 2] = shift - 128 * whole


def pack_kernel(tiles, swapped_ref, edge_ref, packed_ref):
    for i in range(tiles):
        packed_ref[i] = swapped_ref[pl.ds(16 * i + 12, 4), :]
    for a in range(4):
        packed_ref[tiles + a] = edge_ref[a]


def inner_kernel(
    times,
    fields,
    state_ref,
    coeff_ref,
    jac_ref,
    omega_ref,
    _,
    partial_ref,
    mix_ref,
):
    lane = lax.broadcasted_iota(jnp.int32, (8, 128), 1)
    sub = lax.broadcasted_iota(jnp.int32, (8, 128), 0)
    lower = sub < 4
    bottom = sub % 4 == 0
    top = sub % 4 == 3
    coeff = [0.1 * coeff_ref[0:8, :], 0.1 * coeff_ref[8:16, :]]
    own = [0.8 - 4.0 * c for c in coeff]
    rate = -0.1 * omega_ref[0]
    weight = [0.0]
    weight += [0.5 * (-1.0) ** m / math.sin(math.pi * m / times) for m in range(1, times)]

    field = (lane // 2) % fields
    sign = jnp.where(lane % 2 == 0, -0.05, 0.05)
    for distance in range(1 - fields, fields):
        mix = jnp.zeros((8, 128), jnp.float32)
        for f in range(max(0, distance), min(fields, fields + distance)):
            mix = jnp.where(field == f, jac_ref[f, f - distance], mix)
        mix_ref[fields - 1 + distance] = sign * mix

    def step(t, _):
        def load(u, f, h):
            start = pl.multiple_of((u * fields + f) * 16 + 8 * h, 8)
            return state_ref[pl.ds(start, 8), :]

        difference, result = [], []
        for f in range(fields):
            v0, v1 = load(t, f, 0), load(t, f, 1)
            r0, r1 = pltpu.roll(v0, 4, 0), pltpu.roll(v1, 4, 0)
            middle = jnp.where(lower, r0, r1)
            axial = [middle + jnp.where(lower, 0.0, r0), jnp.where(lower, r1, 0.0) + middle]
            differences, results = [], []
            for h, v in enumerate((v0, v1)):
                plus = jnp.where(lane == 127, 0.0, pltpu.roll(v, 127, 1))
                minus = jnp.where(lane == 0, 0.0, pltpu.roll(v, 1, 1))
                up = jnp.where(top, 0.0, pltpu.roll(v, 7, 0))
                down = jnp.where(bottom, 0.0, pltpu.roll(v, 1, 0))
                differences.append(plus - minus)
                value = own[h] * v + coeff[h] * ((plus + minus) + (up + down)) + 0.1 * axial[h]
                spectral = jnp.zeros_like(v)
                for m in range(1, times // 2 + 1):
                    before = load(lax.rem(t + times - m, times), f, h)
                    after = load(lax.rem(t + m, times), f, h)
                    spectral = spectral + weight[m] * (before - after)
                results.append(value + rate * spectral)
            difference.append(differences)
            result.append(results)
        for f in range(fields):
            for h in range(2):
                value = result[f][h]
                for g in range(fields):
                    value = value + (-0.05 * jac_ref[f, g]) * difference[g][h]
                start = pl.multiple_of((t * fields + f) * 16 + 8 * h, 8)
                partial_ref[pl.ds(start, 8), :] = value
        return 0

    lax.fori_loop(0, times, step, 0)


def outer_kernel(
    times,
    fields,
    slots,
    partial_ref,
    mix_ref,
    place_ref,
    coeff_ref,
    even_ref,
    odd_ref,
    edge_a_ref,
    edge_b_ref,
    *rest,
):
    source_refs, (out_ref, span_ref, total_ref, sems) = rest[:-4], rest[-4:]
    tiles = times * fields
    sec_parity = lax.rem(lax.axis_index("sec"), 2)
    span_parity = lax.rem(lax.axis_index("span"), 2)
    lane = lax.broadcasted_iota(jnp.int32, (8, 128), 1)
    sub = lax.broadcasted_iota(jnp.int32, (8, 128), 0)
    lane4 = lax.broadcasted_iota(jnp.int32, (4, 128), 1)
    border = jnp.logical_or(sub % 4 == 0, sub % 4 == 3)
    lower = sub < 4
    outside = jnp.logical_or(lane == 0, lane == 127)
    sides = lane % 2 == 0

    even, odd = even_ref[...], odd_ref[...]
    coeff_low = 0.1 * coeff_ref[pl.ds(0, 4, stride=4), :]
    coeff_high = 0.1 * coeff_ref[pl.ds(3, 4, stride=4), :]
    up = jnp.where(span_parity == 0, even, odd).reshape(tiles, 4, 128) * coeff_high[None]
    down = jnp.where(span_parity == 0, odd, even).reshape(tiles, 4, 128) * coeff_low[None]
    span_ref[pl.ds(3, 4 * tiles, stride=4), :] = up.reshape(4 * tiles, 128)
    span_ref[pl.ds(0, 4 * tiles, stride=4), :] = down.reshape(4 * tiles, 128)

    edges = []
    for h in range(2):
        edge_a = jnp.concatenate([edge_a_ref[tiles_at] for tiles_at in (2 * h, 2 * h + 1)], axis=0)
        edge_b = jnp.concatenate([edge_b_ref[tiles_at] for tiles_at in (2 * h, 2 * h + 1)], axis=0)
        plus_edge = jnp.where(sec_parity == 0, edge_a, edge_b)
        minus_edge = jnp.where(sec_parity == 0, edge_b, edge_a)
        halo = jnp.where(sides, pltpu.roll(plus_edge, 127, 1), pltpu.roll(minus_edge, 1, 1))
        coeff = 0.1 * coeff_ref[8 * h : 8 * h + 8, :]
        term = jnp.where(sides, coeff[:, 127:128], coeff[:, 0:1]) * halo
        for distance in range(1 - fields, fields):
            term = term + mix_ref[fields - 1 + distance] * pltpu.roll(halo, (2 * distance) % 128, 1)
        edges.append(term)

    def pick(slot, index):
        if len(source_refs) == 1:
            return source_refs[0][slot, index]
        value = source_refs[0][index]
        for other in range(1, slots):
            value = jnp.where(slot == other, source_refs[other][index], value)
        return value

    def piece(t):
        rows = pl.ds(pl.multiple_of(t * fields * 16, 16), fields * 16)
        return pltpu.make_async_copy(total_ref.at[rows, :], out_ref.at[rows, :], sems.at[t])

    def step(t, _):
        near, far, part = place_ref[3 * t], place_ref[3 * t + 1], place_ref[3 * t + 2]
        for f in range(fields):
            index = t * fields + f
            ghost = jnp.where(lane4 >= 128 - part, pick(far, index), pick(near, index))
            ghost = pltpu.roll(ghost, part, 1)
            ghost = jnp.concatenate([ghost, ghost], axis=0)
            for h in range(2):
                rows = pl.ds(pl.multiple_of(index * 16 + 8 * h, 8), 8)
                value = partial_ref[rows, :] + jnp.where(border, span_ref[rows, :], 0.0)
                value = value + jnp.where(outside, pltpu.roll(edges[h], 127 - 2 * index, 1), 0.0)
                if h == 1:
                    value = value + jnp.where(lower, 0.0, 0.1 * ghost)
                total_ref[rows, :] = value
        piece(t).start()
        return 0

    lax.fori_loop(0, times, step, 0)
    for t in range(times):
        piece(t).wait()


def on_device(state, viscosity, jacobian, frequency, offsets):
    _, times, fields, axial, spans, cells = state.shape
    tiles = times * fields
    sectors, slabs = lax.axis_size("sec"), lax.axis_size("span")
    flat = state.reshape(tiles * 16, cells)
    coeff = viscosity.reshape(16, cells)
    f32 = jnp.float32
    swapped = lax.ppermute(flat, "row", [(0, 1), (1, 0)])
    local, edge, even, odd, place = pl.pallas_call(
        lambda *refs: collect_kernel(times, fields, *refs),
        out_shape=[
            pltpu.VMEM((tiles * 16, cells), f32),
            pltpu.VMEM((4, 4, cells), f32),
            pltpu.VMEM((tiles * 4, cells), f32),
            pltpu.VMEM((tiles * 4, cells), f32),
            pltpu.SMEM((3 * times,), jnp.int32),
        ],
        in_specs=[ANY, ANY],
        out_specs=[VMEM] * 4 + [SMEM],
        scratch_shapes=[
            pltpu.SMEM((times,), jnp.int32),
            pltpu.SemaphoreType.DMA((times,)),
            pltpu.SemaphoreType.DMA,
        ],
        compiler_params=LIMIT,
        name="collect",
    )(
        pltpu.with_memory_space_constraint(flat, pltpu.HBM),
        pltpu.with_memory_space_constraint(offsets, pltpu.HBM),
    )
    packed = pl.pallas_call(
        lambda *refs: pack_kernel(tiles, *refs),
        out_shape=pltpu.VMEM((tiles + 4, 4, cells), f32),
        in_specs=[VMEM, VMEM],
        out_specs=VMEM,
        compiler_params=LIMIT,
        name="pack",
    )(swapped, edge)
    even = lax.ppermute(even, ("row", "span"), slab_pairs(slabs, 0))
    odd = lax.ppermute(odd, ("row", "span"), slab_pairs(slabs, 1))
    if sectors == 4:
        near = [
            lax.ppermute(packed, "sec", [(k, k ^ distance) for k in range(sectors)])
            for distance in (1, 2, 3)
        ]
        sources = [packed] + near
        edge_a, edge_b = near[0][tiles:], near[2][tiles:]
    else:
        sources = [lax.all_gather(packed[:tiles], "sec")]
        edge_a = lax.ppermute(edge, "sec", sector_pairs(sectors, 0))
        edge_b = lax.ppermute(edge, "sec", sector_pairs(sectors, 1))
    partial, mix = pl.pallas_call(
        lambda *refs: inner_kernel(times, fields, *refs),
        out_shape=[
            pltpu.VMEM((tiles * 16, cells), f32),
            pltpu.VMEM((2 * fields - 1, 8, cells), f32),
        ],
        in_specs=[VMEM, VMEM, SMEM, SMEM, ANY],
        out_specs=[VMEM, VMEM],
        compiler_params=LIMIT,
        cost_estimate=pl.CostEstimate(
            flops=tiles * 16 * cells * 50, bytes_accessed=tiles * 16 * cells * 8, transcendentals=0
        ),
        name="inner",
    )(local, coeff, jacobian[0], frequency, packed)
    out = pl.pallas_call(
        lambda *refs: outer_kernel(times, fields, sectors, *refs),
        out_shape=jax.ShapeDtypeStruct(flat.shape, f32),
        in_specs=[VMEM, VMEM, SMEM] + [VMEM] * (5 + len(sources)),
        out_specs=ANY,
        scratch_shapes=[
            pltpu.VMEM((tiles * 16, cells), f32),
            pltpu.VMEM((tiles * 16, cells), f32),
            pltpu.SemaphoreType.DMA((times,)),
        ],
        compiler_params=LIMIT,
        name="outer",
    )(partial, mix, place, coeff, even, odd, edge_a, edge_b, *sources)
    return out.reshape(state.shape)


def solution(mesh):
    return jax.shard_map(
        on_device,
        mesh=mesh,
        in_specs=(
            P("row", None, None, None, "span", "sec"),
            P("row", None, "span", "sec"),
            P("row", None, None),
            P("row"),
            P(),
        ),
        out_specs=P("row", None, None, None, "span", "sec"),
        check_vma=False,
    )
```

```python
import math

import jax
import jax.numpy as jnp
from jax import lax
from jax.experimental import pallas as pl
from jax.experimental.pallas import tpu as pltpu
from jax.sharding import PartitionSpec as P

VMEM = pl.BlockSpec(memory_space=pltpu.VMEM)
SMEM = pl.BlockSpec(memory_space=pltpu.SMEM)
ANY = pl.BlockSpec(memory_space=pl.ANY)
LIMIT = pltpu.CompilerParams(vmem_limit_bytes=32 * 1024 * 1024)


def sector_pairs(count, first):
    return [
        pair
        for low in range(first, count, 2)
        for pair in ((low, (low + 1) % count), ((low + 1) % count, low))
    ]


def slab_pairs(count, first):
    route = []
    for row in range(2):
        for here in range(count):
            there = here ^ 1 if first == 0 else ((here - 1) ^ 1) + 1
            if 0 <= there < count:
                route.append((row * count + here, row * count + there))
            else:
                route.append((row * count + here, (1 - row) * count + here))
    return route


def collect_kernel(
    times,
    fields,
    source_ref,
    coeff_source_ref,
    jac_source_ref,
    offset_source_ref,
    state_ref,
    edge_ref,
    coeff_ref,
    jac_ref,
    place_ref,
    size_ref,
    offset_ref,
    sems,
    small_sems,
):
    block_rows = fields * 16
    small = [
        pltpu.make_async_copy(source, target, small_sems.at[n])
        for n, (source, target) in enumerate(
            (
                (offset_source_ref, offset_ref),
                (coeff_source_ref, coeff_ref),
                (jac_source_ref, jac_ref),
            )
        )
    ]

    def piece(t):
        rows = pl.ds(t * block_rows, block_rows)
        return pltpu.make_async_copy(source_ref.at[rows, :], state_ref.at[rows, :], sems.at[t])

    for t in range(times):
        piece(t).start()
    for copy in small:
        copy.start()
    lane = lax.broadcasted_iota(jnp.int32, (16, 128), 1)
    edge = jnp.zeros((16, 128), jnp.float32)
    for t in range(times):
        piece(t).wait()
        for f in range(fields):
            i = t * fields + f
            block = state_ref[pl.ds(16 * i, 16), :]
            here = jnp.logical_or(lane == 2 * i, lane == 2 * i + 1)
            edge = jnp.where(here, pltpu.roll(block, 2 * i + 1, 1), edge)
    for a in range(4):
        edge_ref[a] = edge[4 * a : 4 * a + 4]

    for copy in small:
        copy.wait()
    sectors = lax.axis_size("sec")
    row, sec = lax.axis_index("row"), lax.axis_index("sec")
    places = []
    for t in range(times):
        offset = offset_ref[t]
        cut = jnp.bitwise_and(offset, 127)
        whole = jnp.where(row == 0, offset >> 7, sectors - 1 - (offset >> 7))
        near = jnp.where(sec >= whole, sec - whole, sec - whole + sectors)
        far = jnp.where(near > 0, near - 1, sectors - 1)
        place_ref[5 * t + 4] = jnp.where(row == 0, cut, 128 - cut)
        if sectors != 4:
            place_ref[5 * t] = near
            place_ref[5 * t + 1] = t
            place_ref[5 * t + 2] = far
            place_ref[5 * t + 3] = t
        else:
            place_ref[5 * t] = near ^ sec
            place_ref[5 * t + 2] = far ^ sec
            places.append(whole)
    if sectors == 4:
        used = [jnp.int32(0)] * 4
        for t, whole in enumerate(places):
            after = (whole + 1) & 3
            near_place, far_place = jnp.int32(0), jnp.int32(0)
            for ahead in range(1, 4):
                near_place = jnp.where(whole == ahead, used[ahead], near_place)
                far_place = jnp.where(after == ahead, used[ahead], far_place)
                place_ref[(4 + ahead) * times + used[ahead]] = t
                wanted = jnp.logical_or(whole == ahead, after == ahead)
                used[ahead] = used[ahead] + wanted.astype(jnp.int32)
            place_ref[5 * t + 1] = near_place
            place_ref[5 * t + 3] = far_place
        largest = jnp.maximum(jnp.maximum(used[1], used[2]), used[3])
        size_ref[0] = largest - (times + 1) // 2
    else:
        size_ref[0] = 0


def span_kernel(state_ref, even_ref, odd_ref):
    slab, slabs = lax.axis_index("span"), lax.axis_size("span")
    parity = lax.rem(slab, 2)
    paired_even = (slab ^ 1) < slabs
    paired_odd = jnp.logical_and(slab > 0, ((slab - 1) ^ 1) + 1 < slabs)
    low = state_ref[pl.ds(0, state_ref.shape[0] // 4, stride=4), :]
    high = state_ref[pl.ds(3, state_ref.shape[0] // 4, stride=4), :]
    even_ref[...] = jnp.where(paired_even, jnp.where(parity == 0, high, low), 0.0)
    odd_ref[...] = jnp.where(paired_odd, jnp.where(parity == 0, low, high), 0.0)


def pack_kernel(
    times,
    fields,
    held,
    swapped_ref,
    edge_ref,
    place_ref,
    state_ref,
    x_ref,
    y_ref,
    d_ref,
    even_ref,
    odd_ref,
):
    even = lax.rem(lax.axis_index("sec"), 2) == 0
    for distance, packed_ref in ((1, x_ref), (2, y_ref), (3, d_ref)):
        ahead = jnp.int32(2)
        if distance != 2:
            ahead = jnp.where(even, distance, 4 - distance)
        for j in range(held):
            t = place_ref[(4 + ahead) * times + j]
            for f in range(fields):
                start = (t * fields + f) * 16 + 12
                packed_ref[j * fields + f] = swapped_ref[pl.ds(start, 4), :]
        if distance != 2:
            for a in range(4):
                packed_ref[held * fields + a] = edge_ref[a]
    span_kernel(state_ref, even_ref, odd_ref)


def inner_kernel(
    times,
    fields,
    state_ref,
    coeff_ref,
    jac_ref,
    omega_ref,
    _,
    partial_ref,
    mix_ref,
):
    lane = lax.broadcasted_iota(jnp.int32, (8, 128), 1)
    sub = lax.broadcasted_iota(jnp.int32, (8, 128), 0)
    lower = sub < 4
    bottom = sub % 4 == 0
    top = sub % 4 == 3
    coeff = [0.1 * coeff_ref[0:8, :], 0.1 * coeff_ref[8:16, :]]
    own = [0.8 - 4.0 * c for c in coeff]
    rate = -0.1 * omega_ref[0]
    weight = [0.0]
    weight += [0.5 * (-1.0) ** m / math.sin(math.pi * m / times) for m in range(1, times)]

    field = (lane // 2) % fields
    sign = jnp.where(lane % 2 == 0, -0.05, 0.05)
    for distance in range(1 - fields, fields):
        mix = jnp.zeros((8, 128), jnp.float32)
        for f in range(max(0, distance), min(fields, fields + distance)):
            mix = jnp.where(field == f, jac_ref[f, 0, f - distance], mix)
        mix_ref[fields - 1 + distance] = sign * mix

    def step(t, _):
        def load(u, f, h):
            start = pl.multiple_of((u * fields + f) * 16 + 8 * h, 8)
            return state_ref[pl.ds(start, 8), :]

        difference, result = [], []
        for f in range(fields):
            v0, v1 = load(t, f, 0), load(t, f, 1)
            r0, r1 = pltpu.roll(v0, 4, 0), pltpu.roll(v1, 4, 0)
            middle = jnp.where(lower, r0, r1)
            axial = [middle + jnp.where(lower, 0.0, r0), jnp.where(lower, r1, 0.0) + middle]
            differences, results = [], []
            for h, v in enumerate((v0, v1)):
                plus = jnp.where(lane == 127, 0.0, pltpu.roll(v, 127, 1))
                minus = jnp.where(lane == 0, 0.0, pltpu.roll(v, 1, 1))
                up = jnp.where(top, 0.0, pltpu.roll(v, 7, 0))
                down = jnp.where(bottom, 0.0, pltpu.roll(v, 1, 0))
                differences.append(plus - minus)
                value = own[h] * v + coeff[h] * ((plus + minus) + (up + down)) + 0.1 * axial[h]
                spectral = jnp.zeros_like(v)
                for m in range(1, times // 2 + 1):
                    before = load(lax.rem(t + times - m, times), f, h)
                    after = load(lax.rem(t + m, times), f, h)
                    spectral = spectral + weight[m] * (before - after)
                results.append(value + rate * spectral)
            difference.append(differences)
            result.append(results)
        for f in range(fields):
            for h in range(2):
                value = result[f][h]
                for g in range(fields):
                    value = value + (-0.05 * jac_ref[f, 0, g]) * difference[g][h]
                start = pl.multiple_of((t * fields + f) * 16 + 8 * h, 8)
                partial_ref[pl.ds(start, 8), :] = value
        return 0

    lax.fori_loop(0, times, step, 0)


def edge_terms(fields, mix_ref, coeff_ref, edge_a_ref, edge_b_ref):
    even = lax.rem(lax.axis_index("sec"), 2) == 0
    sides = lax.broadcasted_iota(jnp.int32, (8, 128), 1) % 2 == 0
    terms = []
    for h in range(2):
        edge_a = jnp.concatenate([edge_a_ref[2 * h], edge_a_ref[2 * h + 1]], axis=0)
        edge_b = jnp.concatenate([edge_b_ref[2 * h], edge_b_ref[2 * h + 1]], axis=0)
        plus_edge = jnp.where(even, edge_a, edge_b)
        minus_edge = jnp.where(even, edge_b, edge_a)
        halo = jnp.where(sides, pltpu.roll(plus_edge, 127, 1), pltpu.roll(minus_edge, 1, 1))
        coeff = 0.1 * coeff_ref[8 * h : 8 * h + 8, :]
        term = jnp.where(sides, coeff[:, 127:128], coeff[:, 0:1]) * halo
        for distance in range(1 - fields, fields):
            term = term + mix_ref[fields - 1 + distance] * pltpu.roll(halo, (2 * distance) % 128, 1)
        terms.append(term)
    return terms


def sector_kernel(
    times, fields, partial_ref, mix_ref, place_ref, coeff_ref, edge_a_ref, edge_b_ref, *rest
):
    source_refs, total_ref = rest[:-1], rest[-1]
    lane = lax.broadcasted_iota(jnp.int32, (8, 128), 1)
    lower = lax.broadcasted_iota(jnp.int32, (8, 128), 0) < 4
    lane4 = lax.broadcasted_iota(jnp.int32, (4, 128), 1)
    outside = jnp.logical_or(lane == 0, lane == 127)
    edges = edge_terms(fields, mix_ref, coeff_ref, edge_a_ref, edge_b_ref)

    def pick(slot, place, t, f):
        if len(source_refs) == 1:
            return source_refs[0][slot, pl.ds((place * fields + f) * 4, 4), :]
        value = source_refs[0][pl.ds((t * fields + f) * 16 + 12, 4), :]
        for other in range(1, 4):
            value = jnp.where(slot == other, source_refs[other][place * fields + f], value)
        return value

    def step(t, _):
        near, near_place, far, far_place, part = [place_ref[5 * t + n] for n in range(5)]
        for f in range(fields):
            index = t * fields + f
            ghost = jnp.where(
                lane4 >= 128 - part, pick(far, far_place, t, f), pick(near, near_place, t, f)
            )
            ghost = pltpu.roll(ghost, jnp.bitwise_and(part, 127), 1)
            ghost = jnp.concatenate([ghost, ghost], axis=0)
            for h in range(2):
                rows = pl.ds(pl.multiple_of(index * 16 + 8 * h, 8), 8)
                value = partial_ref[rows, :]
                value = value + jnp.where(outside, pltpu.roll(edges[h], 127 - 2 * index, 1), 0.0)
                if h == 1:
                    value = value + jnp.where(lower, 0.0, 0.1 * ghost)
                total_ref[rows, :] = value
        return 0

    lax.fori_loop(0, times, step, 0)


def finish_kernel(
    times, fields, total_ref, coeff_ref, even_ref, odd_ref, out_ref, result_ref, sems
):
    straight = lax.rem(lax.axis_index("span"), 2) == 0
    coeff = []
    for s in (0, 3):
        four = 0.1 * coeff_ref[pl.ds(s, 4, stride=4), :]
        coeff.append(jnp.concatenate([four, four], axis=0))

    def piece(n, first, last):
        rows = pl.ds(first * fields * 16, (last - first) * fields * 16)
        return pltpu.make_async_copy(result_ref.at[rows, :], out_ref.at[rows, :], sems.at[n])

    pieces = [(first, min(first + 2, times)) for first in range(0, times, 2)]
    for n, (first, last) in enumerate(pieces):
        low, high = first * fields * 4, last * fields * 4
        for start in range(low, high, 8):
            size = min(8, high - start)
            even, odd = even_ref[start : start + size, :], odd_ref[start : start + size, :]
            halos = jnp.where(straight, odd, even), jnp.where(straight, even, odd)
            for s, halo, factor in zip((0, 3), halos, coeff):
                rows = pl.ds(4 * start + s, size, stride=4)
                result_ref[rows, :] = total_ref[rows, :] + factor[:size] * halo
        piece(n, first, last).start()
    for n, (first, last) in enumerate(pieces):
        piece(n, first, last).wait()


def exchange(times, fields, held, swapped, local, edge, place, coeff, jacobian, frequency):
    f32 = jnp.float32
    tiles, cells = times * fields, local.shape[1]
    sectors, slabs = lax.axis_size("sec"), lax.axis_size("span")
    if held is None:
        even, odd = pl.pallas_call(
            span_kernel,
            out_shape=[pltpu.VMEM((tiles * 4, cells), f32)] * 2,
            in_specs=[VMEM],
            out_specs=[VMEM] * 2,
            compiler_params=LIMIT,
            name="spans",
        )(local)
        strip = swapped.reshape(tiles, 16, cells)[:, 12:].reshape(tiles * 4, cells)
        sources = [lax.all_gather(strip, "sec")]
        edge_a = lax.ppermute(edge, "sec", sector_pairs(sectors, 0))
        edge_b = lax.ppermute(edge, "sec", sector_pairs(sectors, 1))
        sent = edge
    else:
        *packed, even, odd = pl.pallas_call(
            lambda *refs: pack_kernel(times, fields, held, *refs),
            out_shape=[
                pltpu.VMEM((held * fields + extra, 4, cells), f32) for extra in (4, 0, 4)
            ]
            + [pltpu.VMEM((tiles * 4, cells), f32)] * 2,
            in_specs=[VMEM, VMEM, SMEM, VMEM],
            out_specs=[VMEM] * 5,
            compiler_params=LIMIT,
            name="pack",
        )(swapped, edge, place, local)
        sent = packed[0]
        near = [
            lax.ppermute(block, "sec", [(k, k ^ distance) for k in range(sectors)])
            for distance, block in zip((1, 2, 3), packed)
        ]
        sources = [swapped] + near
        edge_a, edge_b = near[0][held * fields :], near[2][held * fields :]
    even = lax.ppermute(even, ("row", "span"), slab_pairs(slabs, 0))
    odd = lax.ppermute(odd, ("row", "span"), slab_pairs(slabs, 1))
    partial, mix = pl.pallas_call(
        lambda *refs: inner_kernel(times, fields, *refs),
        out_shape=[
            pltpu.VMEM((tiles * 16, cells), f32),
            pltpu.VMEM((2 * fields - 1, 8, cells), f32),
        ],
        in_specs=[VMEM, VMEM, SMEM, SMEM, ANY],
        out_specs=[VMEM, VMEM],
        compiler_params=LIMIT,
        cost_estimate=pl.CostEstimate(
            flops=tiles * 16 * cells * 50000, bytes_accessed=tiles * 16 * cells * 8000, transcendentals=0
        ),
        name="inner",
    )(local, coeff, jacobian, frequency, sent)
    total = pl.pallas_call(
        lambda *refs: sector_kernel(times, fields, *refs),
        out_shape=pltpu.VMEM((tiles * 16, cells), f32),
        in_specs=[VMEM, VMEM, SMEM] + [VMEM] * (3 + len(sources)),
        out_specs=VMEM,
        compiler_params=LIMIT,
        name="sectors",
    )(partial, mix, place, coeff, edge_a, edge_b, *sources)
    out, _ = pl.pallas_call(
        lambda *refs: finish_kernel(times, fields, *refs),
        out_shape=[pltpu.HBM((tiles * 16, cells), f32), pltpu.VMEM((tiles * 16, cells), f32)],
        in_specs=[VMEM] * 4,
        out_specs=[ANY, VMEM],
        scratch_shapes=[pltpu.SemaphoreType.DMA(((times + 1) // 2,))],
        input_output_aliases={0: 1},
        compiler_params=LIMIT,
        name="finish",
    )(total, coeff, even, odd)
    return out


def on_device(state, viscosity, jacobian, frequency, offsets):
    _, times, fields, axial, spans, cells = state.shape
    tiles = times * fields
    sectors, slabs = lax.axis_size("sec"), lax.axis_size("span")
    flat = state.reshape(tiles * 16, cells)
    coeff = viscosity.reshape(16, cells)
    f32 = jnp.float32
    swapped = lax.ppermute(flat, "row", [(0, 1), (1, 0)])
    local, edge, coeff, jac, place, size = pl.pallas_call(
        lambda *refs: collect_kernel(times, fields, *refs),
        out_shape=[
            pltpu.VMEM((tiles * 16, cells), f32),
            pltpu.VMEM((4, 4, cells), f32),
            pltpu.VMEM((16, cells), f32),
            pltpu.SMEM((fields, 1, fields), f32),
            pltpu.SMEM((8 * times,), jnp.int32),
            pltpu.SMEM((1,), jnp.int32),
        ],
        in_specs=[ANY] * 4,
        out_specs=[VMEM] * 3 + [SMEM] * 3,
        scratch_shapes=[
            pltpu.SMEM((times,), jnp.int32),
            pltpu.SemaphoreType.DMA((times,)),
            pltpu.SemaphoreType.DMA((3,)),
        ],
        compiler_params=LIMIT,
        name="collect",
    )(
        *(
            pltpu.with_memory_space_constraint(x, pltpu.HBM)
            for x in (flat, coeff, jnp.swapaxes(jacobian, 0, 1), offsets)
        )
    )
    operands = (swapped, local, edge, place, coeff, jac, frequency)
    if sectors == 4:
        branches = [
            lambda *held_operands, held=held: exchange(times, fields, held, *held_operands)
            for held in range((times + 1) // 2, times + 1)
        ]
        out = lax.switch(size[0], branches, *operands)
    else:
        out = exchange(times, fields, None, *operands)
    return out.reshape(state.shape)


def solution(mesh):
    return jax.shard_map(
        on_device,
        mesh=mesh,
        in_specs=(
            P("row", None, None, None, "span", "sec"),
            P("row", None, "span", "sec"),
            P("row", None, None),
            P("row"),
            P(),
        ),
        out_specs=P("row", None, None, None, "span", "sec"),
        check_vma=False,
    )
```

```python
import math

import jax
import jax.numpy as jnp
from jax import lax
from jax.experimental import pallas as pl
from jax.experimental.pallas import tpu as pltpu
from jax.sharding import PartitionSpec as P

VMEM = pl.BlockSpec(memory_space=pltpu.VMEM)
SMEM = pl.BlockSpec(memory_space=pltpu.SMEM)
ANY = pl.BlockSpec(memory_space=pl.ANY)
LIMIT = pltpu.CompilerParams(vmem_limit_bytes=32 * 1024 * 1024)


def sector_pairs(count, first):
    return [
        pair
        for low in range(first, count, 2)
        for pair in ((low, (low + 1) % count), ((low + 1) % count, low))
    ]


def slab_pairs(count, first):
    route = []
    for row in range(2):
        for here in range(count):
            there = here ^ 1 if first == 0 else ((here - 1) ^ 1) + 1
            if 0 <= there < count:
                route.append((row * count + here, row * count + there))
            else:
                route.append((row * count + here, (1 - row) * count + here))
    return route


def collect_kernel(
    times,
    fields,
    source_ref,
    coeff_source_ref,
    jac_source_ref,
    offset_source_ref,
    state_ref,
    edge_ref,
    coeff_ref,
    jac_ref,
    place_ref,
    size_ref,
    offset_ref,
    sems,
    small_sems,
):
    block_rows = fields * 16
    small = [
        pltpu.make_async_copy(source, target, small_sems.at[n])
        for n, (source, target) in enumerate(
            (
                (offset_source_ref, offset_ref),
                (coeff_source_ref, coeff_ref),
                (jac_source_ref, jac_ref),
            )
        )
    ]

    def piece(t):
        rows = pl.ds(t * block_rows, block_rows)
        return pltpu.make_async_copy(source_ref.at[rows, :], state_ref.at[rows, :], sems.at[t])

    for t in range(times):
        piece(t).start()
    for copy in small:
        copy.start()
    lane = lax.broadcasted_iota(jnp.int32, (16, 128), 1)
    edge = jnp.zeros((16, 128), jnp.float32)
    for t in range(times):
        piece(t).wait()
    for t in range(times):
        for f in range(fields):
            i = t * fields + f
            block = state_ref[pl.ds(16 * i, 16), :]
            here = jnp.logical_or(lane == 2 * i, lane == 2 * i + 1)
            edge = jnp.where(here, pltpu.roll(block, 2 * i + 1, 1), edge)
    for a in range(4):
        edge_ref[a] = edge[4 * a : 4 * a + 4]

    for copy in small:
        copy.wait()
    sectors = lax.axis_size("sec")
    row, sec = lax.axis_index("row"), lax.axis_index("sec")
    places = []
    for t in range(times):
        offset = offset_ref[t]
        cut = jnp.bitwise_and(offset, 127)
        whole = jnp.where(row == 0, offset >> 7, sectors - 1 - (offset >> 7))
        near = jnp.where(sec >= whole, sec - whole, sec - whole + sectors)
        far = jnp.where(near > 0, near - 1, sectors - 1)
        place_ref[5 * t + 4] = jnp.where(row == 0, cut, 128 - cut)
        if sectors != 4:
            place_ref[5 * t] = near
            place_ref[5 * t + 1] = t
            place_ref[5 * t + 2] = far
            place_ref[5 * t + 3] = t
        else:
            place_ref[5 * t] = near ^ sec
            place_ref[5 * t + 2] = far ^ sec
            places.append(whole)
    if sectors == 4:
        used = [jnp.int32(0)] * 4
        for t, whole in enumerate(places):
            after = (whole + 1) & 3
            near_place, far_place = jnp.int32(0), jnp.int32(0)
            for ahead in range(1, 4):
                near_place = jnp.where(whole == ahead, used[ahead], near_place)
                far_place = jnp.where(after == ahead, used[ahead], far_place)
                place_ref[(4 + ahead) * times + used[ahead]] = t
                wanted = jnp.logical_or(whole == ahead, after == ahead)
                used[ahead] = used[ahead] + wanted.astype(jnp.int32)
            place_ref[5 * t + 1] = near_place
            place_ref[5 * t + 3] = far_place
        largest = jnp.maximum(jnp.maximum(used[1], used[2]), used[3])
        size_ref[0] = largest - (times + 1) // 2
    else:
        size_ref[0] = 0


def span_kernel(state_ref, even_ref, odd_ref):
    slab, slabs = lax.axis_index("span"), lax.axis_size("span")
    parity = lax.rem(slab, 2)
    paired_even = (slab ^ 1) < slabs
    paired_odd = jnp.logical_and(slab > 0, ((slab - 1) ^ 1) + 1 < slabs)
    low = state_ref[pl.ds(0, state_ref.shape[0] // 4, stride=4), :]
    high = state_ref[pl.ds(3, state_ref.shape[0] // 4, stride=4), :]
    even_ref[...] = jnp.where(paired_even, jnp.where(parity == 0, high, low), 0.0)
    odd_ref[...] = jnp.where(paired_odd, jnp.where(parity == 0, low, high), 0.0)


def pack_kernel(
    times,
    fields,
    held,
    swapped_ref,
    edge_ref,
    place_ref,
    state_ref,
    x_ref,
    y_ref,
    d_ref,
    even_ref,
    odd_ref,
):
    even = lax.rem(lax.axis_index("sec"), 2) == 0
    for distance, packed_ref in ((1, x_ref), (2, y_ref), (3, d_ref)):
        ahead = jnp.int32(2)
        if distance != 2:
            ahead = jnp.where(even, distance, 4 - distance)
        for j in range(held):
            t = place_ref[(4 + ahead) * times + j]
            for f in range(fields):
                start = (t * fields + f) * 16 + 12
                packed_ref[j * fields + f] = swapped_ref[pl.ds(start, 4), :]
        if distance != 2:
            for a in range(4):
                packed_ref[held * fields + a] = edge_ref[a]
    span_kernel(state_ref, even_ref, odd_ref)


def inner_kernel(
    times,
    fields,
    state_ref,
    coeff_ref,
    jac_ref,
    omega_ref,
    _,
    partial_ref,
    mix_ref,
):
    lane = lax.broadcasted_iota(jnp.int32, (8, 128), 1)
    sub = lax.broadcasted_iota(jnp.int32, (8, 128), 0)
    lower = sub < 4
    bottom = sub % 4 == 0
    top = sub % 4 == 3
    coeff = [0.1 * coeff_ref[0:8, :], 0.1 * coeff_ref[8:16, :]]
    own = [0.8 - 4.0 * c for c in coeff]
    rate = -0.1 * omega_ref[0]
    weight = [0.0]
    weight += [0.5 * (-1.0) ** m / math.sin(math.pi * m / times) for m in range(1, times)]

    field = (lane // 2) % fields
    sign = jnp.where(lane % 2 == 0, -0.05, 0.05)
    for distance in range(1 - fields, fields):
        mix = jnp.zeros((8, 128), jnp.float32)
        for f in range(max(0, distance), min(fields, fields + distance)):
            mix = jnp.where(field == f, jac_ref[f, 0, f - distance], mix)
        mix_ref[fields - 1 + distance] = sign * mix

    def step(t, _):
        def load(u, f, h):
            start = pl.multiple_of((u * fields + f) * 16 + 8 * h, 8)
            return state_ref[pl.ds(start, 8), :]

        difference, result = [], []
        for f in range(fields):
            v0, v1 = load(t, f, 0), load(t, f, 1)
            r0, r1 = pltpu.roll(v0, 4, 0), pltpu.roll(v1, 4, 0)
            middle = jnp.where(lower, r0, r1)
            axial = [middle + jnp.where(lower, 0.0, r0), jnp.where(lower, r1, 0.0) + middle]
            differences, results = [], []
            for h, v in enumerate((v0, v1)):
                plus = jnp.where(lane == 127, 0.0, pltpu.roll(v, 127, 1))
                minus = jnp.where(lane == 0, 0.0, pltpu.roll(v, 1, 1))
                up = jnp.where(top, 0.0, pltpu.roll(v, 7, 0))
                down = jnp.where(bottom, 0.0, pltpu.roll(v, 1, 0))
                differences.append(plus - minus)
                value = own[h] * v + coeff[h] * ((plus + minus) + (up + down)) + 0.1 * axial[h]
                spectral = jnp.zeros_like(v)
                for m in range(1, times // 2 + 1):
                    before = load(lax.rem(t + times - m, times), f, h)
                    after = load(lax.rem(t + m, times), f, h)
                    spectral = spectral + weight[m] * (before - after)
                results.append(value + rate * spectral)
            difference.append(differences)
            result.append(results)
        for f in range(fields):
            for h in range(2):
                value = result[f][h]
                for g in range(fields):
                    value = value + (-0.05 * jac_ref[f, 0, g]) * difference[g][h]
                start = pl.multiple_of((t * fields + f) * 16 + 8 * h, 8)
                partial_ref[pl.ds(start, 8), :] = value
        return 0

    lax.fori_loop(0, times, step, 0)


def edge_terms(fields, mix_ref, coeff_ref, edge_a_ref, edge_b_ref):
    even = lax.rem(lax.axis_index("sec"), 2) == 0
    sides = lax.broadcasted_iota(jnp.int32, (8, 128), 1) % 2 == 0
    terms = []
    for h in range(2):
        edge_a = jnp.concatenate([edge_a_ref[2 * h], edge_a_ref[2 * h + 1]], axis=0)
        edge_b = jnp.concatenate([edge_b_ref[2 * h], edge_b_ref[2 * h + 1]], axis=0)
        plus_edge = jnp.where(even, edge_a, edge_b)
        minus_edge = jnp.where(even, edge_b, edge_a)
        halo = jnp.where(sides, pltpu.roll(plus_edge, 127, 1), pltpu.roll(minus_edge, 1, 1))
        coeff = 0.1 * coeff_ref[8 * h : 8 * h + 8, :]
        term = jnp.where(sides, coeff[:, 127:128], coeff[:, 0:1]) * halo
        for distance in range(1 - fields, fields):
            term = term + mix_ref[fields - 1 + distance] * pltpu.roll(halo, (2 * distance) % 128, 1)
        terms.append(term)
    return terms


def sector_kernel(
    times, fields, partial_ref, mix_ref, place_ref, coeff_ref, edge_a_ref, edge_b_ref, *rest
):
    source_refs, total_ref = rest[:-1], rest[-1]
    lane = lax.broadcasted_iota(jnp.int32, (8, 128), 1)
    lower = lax.broadcasted_iota(jnp.int32, (8, 128), 0) < 4
    lane4 = lax.broadcasted_iota(jnp.int32, (4, 128), 1)
    outside = jnp.logical_or(lane == 0, lane == 127)
    edges = edge_terms(fields, mix_ref, coeff_ref, edge_a_ref, edge_b_ref)

    def pick(slot, place, t, f):
        if len(source_refs) == 1:
            return source_refs[0][slot, pl.ds((place * fields + f) * 4, 4), :]
        value = source_refs[0][pl.ds((t * fields + f) * 16 + 12, 4), :]
        for other in range(1, 4):
            value = jnp.where(slot == other, source_refs[other][place * fields + f], value)
        return value

    def step(t, _):
        near, near_place, far, far_place, part = [place_ref[5 * t + n] for n in range(5)]
        for f in range(fields):
            index = t * fields + f
            ghost = jnp.where(
                lane4 >= 128 - part, pick(far, far_place, t, f), pick(near, near_place, t, f)
            )
            ghost = pltpu.roll(ghost, jnp.bitwise_and(part, 127), 1)
            ghost = jnp.concatenate([ghost, ghost], axis=0)
            for h in range(2):
                rows = pl.ds(pl.multiple_of(index * 16 + 8 * h, 8), 8)
                value = partial_ref[rows, :]
                value = value + jnp.where(outside, pltpu.roll(edges[h], 127 - 2 * index, 1), 0.0)
                if h == 1:
                    value = value + jnp.where(lower, 0.0, 0.1 * ghost)
                total_ref[rows, :] = value
        return 0

    lax.fori_loop(0, times, step, 0, unroll=9)


def finish_kernel(
    times, fields, total_ref, coeff_ref, even_ref, odd_ref, out_ref, result_ref, sems
):
    straight = lax.rem(lax.axis_index("span"), 2) == 0
    coeff = []
    for s in (0, 3):
        four = 0.1 * coeff_ref[pl.ds(s, 4, stride=4), :]
        coeff.append(jnp.concatenate([four, four], axis=0))

    def piece(n, first, last):
        rows = pl.ds(first * fields * 16, (last - first) * fields * 16)
        return pltpu.make_async_copy(result_ref.at[rows, :], out_ref.at[rows, :], sems.at[n])

    pieces = [(first, min(first + 2, times)) for first in range(0, times, 2)]
    for n, (first, last) in enumerate(pieces):
        low, high = first * fields * 4, last * fields * 4
        for start in range(low, high, 8):
            size = min(8, high - start)
            even, odd = even_ref[start : start + size, :], odd_ref[start : start + size, :]
            halos = jnp.where(straight, odd, even), jnp.where(straight, even, odd)
            for s, halo, factor in zip((0, 3), halos, coeff):
                rows = pl.ds(4 * start + s, size, stride=4)
                result_ref[rows, :] = total_ref[rows, :] + factor[:size] * halo
        piece(n, first, last).start()
    for n, (first, last) in enumerate(pieces):
        piece(n, first, last).wait()


def exchange(times, fields, held, swapped, local, edge, place, coeff, jacobian, frequency):
    f32 = jnp.float32
    tiles, cells = times * fields, local.shape[1]
    sectors, slabs = lax.axis_size("sec"), lax.axis_size("span")
    if held is None:
        even, odd = pl.pallas_call(
            span_kernel,
            out_shape=[pltpu.VMEM((tiles * 4, cells), f32)] * 2,
            in_specs=[VMEM],
            out_specs=[VMEM] * 2,
            compiler_params=LIMIT,
            name="spans",
        )(local)
        strip = swapped.reshape(tiles, 16, cells)[:, 12:].reshape(tiles * 4, cells)
        sources = [lax.all_gather(strip, "sec")]
        edge_a = lax.ppermute(edge, "sec", sector_pairs(sectors, 0))
        edge_b = lax.ppermute(edge, "sec", sector_pairs(sectors, 1))
        sent = edge
    else:
        *packed, even, odd = pl.pallas_call(
            lambda *refs: pack_kernel(times, fields, held, *refs),
            out_shape=[
                pltpu.VMEM((held * fields + extra, 4, cells), f32) for extra in (4, 0, 4)
            ]
            + [pltpu.VMEM((tiles * 4, cells), f32)] * 2,
            in_specs=[VMEM, VMEM, SMEM, VMEM],
            out_specs=[VMEM] * 5,
            compiler_params=LIMIT,
            name="pack",
        )(swapped, edge, place, local)
        sent = packed[0]
        near = [
            lax.ppermute(block, "sec", [(k, k ^ distance) for k in range(sectors)])
            for distance, block in zip((1, 2, 3), packed)
        ]
        sources = [swapped] + near
        edge_a, edge_b = near[0][held * fields :], near[2][held * fields :]
    even = lax.ppermute(even, ("row", "span"), slab_pairs(slabs, 0))
    odd = lax.ppermute(odd, ("row", "span"), slab_pairs(slabs, 1))
    partial, mix = pl.pallas_call(
        lambda *refs: inner_kernel(times, fields, *refs),
        out_shape=[
            pltpu.VMEM((tiles * 16, cells), f32),
            pltpu.VMEM((2 * fields - 1, 8, cells), f32),
        ],
        in_specs=[VMEM, VMEM, SMEM, SMEM, ANY],
        out_specs=[VMEM, VMEM],
        compiler_params=LIMIT,
        cost_estimate=pl.CostEstimate(
            flops=tiles * 16 * cells * 50000, bytes_accessed=tiles * 16 * cells * 8000, transcendentals=0
        ),
        name="inner",
    )(local, coeff, jacobian, frequency, sent)
    total = pl.pallas_call(
        lambda *refs: sector_kernel(times, fields, *refs),
        out_shape=pltpu.VMEM((tiles * 16, cells), f32),
        in_specs=[VMEM, VMEM, SMEM] + [VMEM] * (3 + len(sources)),
        out_specs=VMEM,
        compiler_params=LIMIT,
        name="sectors",
    )(partial, mix, place, coeff, edge_a, edge_b, *sources)
    out, _ = pl.pallas_call(
        lambda *refs: finish_kernel(times, fields, *refs),
        out_shape=[pltpu.HBM((tiles * 16, cells), f32), pltpu.VMEM((tiles * 16, cells), f32)],
        in_specs=[VMEM] * 4,
        out_specs=[ANY, VMEM],
        scratch_shapes=[pltpu.SemaphoreType.DMA(((times + 1) // 2,))],
        input_output_aliases={0: 1},
        compiler_params=LIMIT,
        name="finish",
    )(total, coeff, even, odd)
    return out


def on_device(state, viscosity, jacobian, frequency, offsets):
    _, times, fields, axial, spans, cells = state.shape
    tiles = times * fields
    sectors, slabs = lax.axis_size("sec"), lax.axis_size("span")
    flat = state.reshape(tiles * 16, cells)
    coeff = viscosity.reshape(16, cells)
    f32 = jnp.float32
    swapped = lax.ppermute(flat, "row", [(0, 1), (1, 0)])
    local, edge, coeff, jac, place, size = pl.pallas_call(
        lambda *refs: collect_kernel(times, fields, *refs),
        out_shape=[
            pltpu.VMEM((tiles * 16, cells), f32),
            pltpu.VMEM((4, 4, cells), f32),
            pltpu.VMEM((16, cells), f32),
            pltpu.SMEM((fields, 1, fields), f32),
            pltpu.SMEM((8 * times,), jnp.int32),
            pltpu.SMEM((1,), jnp.int32),
        ],
        in_specs=[ANY] * 4,
        out_specs=[VMEM] * 3 + [SMEM] * 3,
        scratch_shapes=[
            pltpu.SMEM((times,), jnp.int32),
            pltpu.SemaphoreType.DMA((times,)),
            pltpu.SemaphoreType.DMA((3,)),
        ],
        compiler_params=LIMIT,
        name="collect",
    )(
        *(
            pltpu.with_memory_space_constraint(x, pltpu.HBM)
            for x in (flat, coeff, jnp.swapaxes(jacobian, 0, 1), offsets)
        )
    )
    operands = (swapped, local, edge, place, coeff, jac, frequency)
    if sectors == 4:
        branches = [
            lambda *held_operands, held=held: exchange(times, fields, held, *held_operands)
            for held in range((times + 1) // 2, times + 1)
        ]
        out = lax.switch(size[0], branches, *operands)
    else:
        out = exchange(times, fields, None, *operands)
    return out.reshape(state.shape)


def solution(mesh):
    return jax.shard_map(
        on_device,
        mesh=mesh,
        in_specs=(
            P("row", None, None, None, "span", "sec"),
            P("row", None, "span", "sec"),
            P("row", None, None),
            P("row"),
            P(),
        ),
        out_specs=P("row", None, None, None, "span", "sec"),
        check_vma=False,
    )
```

```python
import math

import jax
import jax.numpy as jnp
from jax import lax
from jax.experimental import pallas as pl
from jax.experimental.pallas import tpu as pltpu
from jax.sharding import PartitionSpec as P

VMEM = pl.BlockSpec(memory_space=pltpu.VMEM)
SMEM = pl.BlockSpec(memory_space=pltpu.SMEM)
ANY = pl.BlockSpec(memory_space=pl.ANY)
LIMIT = pltpu.CompilerParams(vmem_limit_bytes=32 * 1024 * 1024)


def sector_pairs(count, first):
    return [
        pair
        for low in range(first, count, 2)
        for pair in ((low, (low + 1) % count), ((low + 1) % count, low))
    ]


def slab_pairs(count, first):
    route = []
    for row in range(2):
        for here in range(count):
            there = here ^ 1 if first == 0 else ((here - 1) ^ 1) + 1
            if 0 <= there < count:
                route.append((row * count + here, row * count + there))
            else:
                route.append((row * count + here, (1 - row) * count + here))
    return route


def collect_kernel(
    times,
    fields,
    source_ref,
    coeff_source_ref,
    jac_source_ref,
    offset_source_ref,
    state_ref,
    edge_ref,
    coeff_ref,
    jac_ref,
    place_ref,
    size_ref,
    offset_ref,
    sems,
    small_sems,
):
    block_rows = fields * 16
    small = [
        pltpu.make_async_copy(source, target, small_sems.at[n])
        for n, (source, target) in enumerate(
            (
                (offset_source_ref, offset_ref),
                (coeff_source_ref, coeff_ref),
                (jac_source_ref, jac_ref),
            )
        )
    ]

    def piece(t):
        rows = pl.ds(t * block_rows, block_rows)
        return pltpu.make_async_copy(source_ref.at[rows, :], state_ref.at[rows, :], sems.at[t])

    for t in range(times):
        piece(t).start()
    for copy in small:
        copy.start()
    lane = lax.broadcasted_iota(jnp.int32, (16, 128), 1)
    edge = jnp.zeros((16, 128), jnp.float32)
    for t in range(times):
        piece(t).wait()
    for t in range(times):
        for f in range(fields):
            i = t * fields + f
            block = state_ref[pl.ds(16 * i, 16), :]
            here = jnp.logical_or(lane == 2 * i, lane == 2 * i + 1)
            edge = jnp.where(here, pltpu.roll(block, 2 * i + 1, 1), edge)
    for a in range(4):
        edge_ref[a] = edge[4 * a : 4 * a + 4]

    for copy in small:
        copy.wait()
    sectors = lax.axis_size("sec")
    row, sec = lax.axis_index("row"), lax.axis_index("sec")
    places = []
    for t in range(times):
        offset = offset_ref[t]
        cut = jnp.bitwise_and(offset, 127)
        whole = jnp.where(row == 0, offset >> 7, sectors - 1 - (offset >> 7))
        near = jnp.where(sec >= whole, sec - whole, sec - whole + sectors)
        far = jnp.where(near > 0, near - 1, sectors - 1)
        place_ref[5 * t + 4] = jnp.where(row == 0, cut, 128 - cut)
        if sectors != 4:
            place_ref[5 * t] = near
            place_ref[5 * t + 1] = t
            place_ref[5 * t + 2] = far
            place_ref[5 * t + 3] = t
        else:
            place_ref[5 * t] = near ^ sec
            place_ref[5 * t + 2] = far ^ sec
            places.append(whole)
    if sectors == 4:
        used = [jnp.int32(0)] * 4
        for t, whole in enumerate(places):
            after = (whole + 1) & 3
            near_place, far_place = jnp.int32(0), jnp.int32(0)
            for ahead in range(1, 4):
                near_place = jnp.where(whole == ahead, used[ahead], near_place)
                far_place = jnp.where(after == ahead, used[ahead], far_place)
                place_ref[(4 + ahead) * times + used[ahead]] = t
                wanted = jnp.logical_or(whole == ahead, after == ahead)
                used[ahead] = used[ahead] + wanted.astype(jnp.int32)
            place_ref[5 * t + 1] = near_place
            place_ref[5 * t + 3] = far_place
        largest = jnp.maximum(jnp.maximum(used[1], used[2]), used[3])
        size_ref[0] = largest - (times + 1) // 2
    else:
        size_ref[0] = 0


def span_kernel(state_ref, even_ref, odd_ref):
    slab, slabs = lax.axis_index("span"), lax.axis_size("span")
    parity = lax.rem(slab, 2)
    paired_even = (slab ^ 1) < slabs
    paired_odd = jnp.logical_and(slab > 0, ((slab - 1) ^ 1) + 1 < slabs)
    low = state_ref[pl.ds(0, state_ref.shape[0] // 4, stride=4), :]
    high = state_ref[pl.ds(3, state_ref.shape[0] // 4, stride=4), :]
    even_ref[: low.shape[0], :] = jnp.where(paired_even, jnp.where(parity == 0, high, low), 0.0)
    odd_ref[: low.shape[0], :] = jnp.where(paired_odd, jnp.where(parity == 0, low, high), 0.0)


def pack_kernel(
    times,
    fields,
    held,
    swapped_ref,
    edge_ref,
    place_ref,
    state_ref,
    x_ref,
    y_ref,
    d_ref,
    even_ref,
    odd_ref,
):
    even = lax.rem(lax.axis_index("sec"), 2) == 0
    for distance, packed_ref in ((1, x_ref), (2, y_ref), (3, d_ref)):
        ahead = jnp.int32(2)
        if distance != 2:
            ahead = jnp.where(even, distance, 4 - distance)
        for j in range(held):
            t = place_ref[(4 + ahead) * times + j]
            for f in range(fields):
                start = (t * fields + f) * 16 + 12
                packed_ref[j * fields + f] = swapped_ref[pl.ds(start, 4), :]
        if distance != 2:
            for a in range(4):
                packed_ref[held * fields + a] = edge_ref[a]
    span_kernel(state_ref, even_ref, odd_ref)


def inner_kernel(
    times,
    fields,
    state_ref,
    coeff_ref,
    jac_ref,
    omega_ref,
    _,
    partial_ref,
    mix_ref,
):
    lane = lax.broadcasted_iota(jnp.int32, (8, 128), 1)
    sub = lax.broadcasted_iota(jnp.int32, (8, 128), 0)
    lower = sub < 4
    bottom = sub % 4 == 0
    top = sub % 4 == 3
    coeff = [0.1 * coeff_ref[0:8, :], 0.1 * coeff_ref[8:16, :]]
    own = [0.8 - 4.0 * c for c in coeff]
    rate = -0.1 * omega_ref[0]
    weight = [0.0]
    weight += [0.5 * (-1.0) ** m / math.sin(math.pi * m / times) for m in range(1, times)]

    field = (lane // 2) % fields
    sign = jnp.where(lane % 2 == 0, -0.05, 0.05)
    for distance in range(1 - fields, fields):
        mix = jnp.zeros((8, 128), jnp.float32)
        for f in range(max(0, distance), min(fields, fields + distance)):
            mix = jnp.where(field == f, jac_ref[f, 0, f - distance], mix)
        mix_ref[fields - 1 + distance] = sign * mix

    def step(t, _):
        def load(u, f, h):
            start = pl.multiple_of((u * fields + f) * 16 + 8 * h, 8)
            return state_ref[pl.ds(start, 8), :]

        difference, result = [], []
        for f in range(fields):
            v0, v1 = load(t, f, 0), load(t, f, 1)
            r0, r1 = pltpu.roll(v0, 4, 0), pltpu.roll(v1, 4, 0)
            middle = jnp.where(lower, r0, r1)
            axial = [middle + jnp.where(lower, 0.0, r0), jnp.where(lower, r1, 0.0) + middle]
            differences, results = [], []
            for h, v in enumerate((v0, v1)):
                plus = jnp.where(lane == 127, 0.0, pltpu.roll(v, 127, 1))
                minus = jnp.where(lane == 0, 0.0, pltpu.roll(v, 1, 1))
                up = jnp.where(top, 0.0, pltpu.roll(v, 7, 0))
                down = jnp.where(bottom, 0.0, pltpu.roll(v, 1, 0))
                differences.append(plus - minus)
                value = own[h] * v + coeff[h] * ((plus + minus) + (up + down)) + 0.1 * axial[h]
                spectral = jnp.zeros_like(v)
                for m in range(1, times // 2 + 1):
                    before = load(lax.rem(t + times - m, times), f, h)
                    after = load(lax.rem(t + m, times), f, h)
                    spectral = spectral + weight[m] * (before - after)
                results.append(value + rate * spectral)
            difference.append(differences)
            result.append(results)
        for f in range(fields):
            for h in range(2):
                value = result[f][h]
                for g in range(fields):
                    value = value + (-0.05 * jac_ref[f, 0, g]) * difference[g][h]
                start = pl.multiple_of((t * fields + f) * 16 + 8 * h, 8)
                partial_ref[pl.ds(start, 8), :] = value
        return 0

    lax.fori_loop(0, times, step, 0)


def edge_terms(fields, mix_ref, coeff_ref, edge_a_ref, edge_b_ref):
    even = lax.rem(lax.axis_index("sec"), 2) == 0
    sides = lax.broadcasted_iota(jnp.int32, (8, 128), 1) % 2 == 0
    terms = []
    for h in range(2):
        edge_a = jnp.concatenate([edge_a_ref[2 * h], edge_a_ref[2 * h + 1]], axis=0)
        edge_b = jnp.concatenate([edge_b_ref[2 * h], edge_b_ref[2 * h + 1]], axis=0)
        plus_edge = jnp.where(even, edge_a, edge_b)
        minus_edge = jnp.where(even, edge_b, edge_a)
        halo = jnp.where(sides, pltpu.roll(plus_edge, 127, 1), pltpu.roll(minus_edge, 1, 1))
        coeff = 0.1 * coeff_ref[8 * h : 8 * h + 8, :]
        term = jnp.where(sides, coeff[:, 127:128], coeff[:, 0:1]) * halo
        for distance in range(1 - fields, fields):
            term = term + mix_ref[fields - 1 + distance] * pltpu.roll(halo, (2 * distance) % 128, 1)
        terms.append(term)
    return terms


def sector_kernel(
    times, fields, partial_ref, mix_ref, place_ref, coeff_ref, edge_a_ref, edge_b_ref, *rest
):
    source_refs, total_ref = rest[:-1], rest[-1]
    lane = lax.broadcasted_iota(jnp.int32, (8, 128), 1)
    lower = lax.broadcasted_iota(jnp.int32, (8, 128), 0) < 4
    lane4 = lax.broadcasted_iota(jnp.int32, (4, 128), 1)
    outside = jnp.logical_or(lane == 0, lane == 127)
    edges = edge_terms(fields, mix_ref, coeff_ref, edge_a_ref, edge_b_ref)

    def pick(slot, place, t, f):
        if len(source_refs) == 1:
            return source_refs[0][slot, pl.ds((place * fields + f) * 4, 4), :]
        value = source_refs[0][pl.ds((t * fields + f) * 16 + 12, 4), :]
        for other in range(1, 4):
            value = jnp.where(slot == other, source_refs[other][place * fields + f], value)
        return value

    def step(t, _):
        near, near_place, far, far_place, part = [place_ref[5 * t + n] for n in range(5)]
        for f in range(fields):
            index = t * fields + f
            ghost = jnp.where(
                lane4 >= 128 - part, pick(far, far_place, t, f), pick(near, near_place, t, f)
            )
            ghost = pltpu.roll(ghost, jnp.bitwise_and(part, 127), 1)
            ghost = jnp.concatenate([ghost, ghost], axis=0)
            for h in range(2):
                rows = pl.ds(pl.multiple_of(index * 16 + 8 * h, 8), 8)
                value = partial_ref[rows, :]
                value = value + jnp.where(outside, pltpu.roll(edges[h], 127 - 2 * index, 1), 0.0)
                if h == 1:
                    value = value + jnp.where(lower, 0.0, 0.1 * ghost)
                total_ref[rows, :] = value
        return 0

    lax.fori_loop(0, times, step, 0, unroll=9)


def finish_kernel(
    times, fields, total_ref, coeff_ref, even_ref, odd_ref, out_ref, result_ref, sems
):
    straight = lax.rem(lax.axis_index("span"), 2) == 0
    coeff = []
    for s in (0, 3):
        four = 0.1 * coeff_ref[pl.ds(s, 4, stride=4), :]
        coeff.append(jnp.concatenate([four, four], axis=0))

    def piece(n, first, last):
        rows = pl.ds(first * fields * 16, (last - first) * fields * 16)
        return pltpu.make_async_copy(result_ref.at[rows, :], out_ref.at[rows, :], sems.at[n])

    pieces = [(first, min(first + 2, times)) for first in range(0, times, 2)]
    for n, (first, last) in enumerate(pieces):
        low, high = first * fields * 4, last * fields * 4
        for start in range(low, high, 8):
            size = min(8, high - start)
            even, odd = even_ref[start : start + size, :], odd_ref[start : start + size, :]
            halos = jnp.where(straight, odd, even), jnp.where(straight, even, odd)
            for s, halo, factor in zip((0, 3), halos, coeff):
                rows = pl.ds(4 * start + s, size, stride=4)
                result_ref[rows, :] = total_ref[rows, :] + factor[:size] * halo
        piece(n, first, last).start()
    for n, (first, last) in enumerate(pieces):
        piece(n, first, last).wait()


def exchange(times, fields, held, swapped, local, edge, place, coeff, jacobian, frequency):
    f32 = jnp.float32
    tiles, cells = times * fields, local.shape[1]
    sectors, slabs = lax.axis_size("sec"), lax.axis_size("span")
    if held is None:
        even, odd = pl.pallas_call(
            span_kernel,
            out_shape=[pltpu.VMEM((tiles * 4, cells), f32)] * 2,
            in_specs=[VMEM],
            out_specs=[VMEM] * 2,
            compiler_params=LIMIT,
            name="spans",
        )(local)
        strip = swapped.reshape(tiles, 16, cells)[:, 12:].reshape(tiles * 4, cells)
        sources = [lax.all_gather(strip, "sec")]
        edge_a = lax.ppermute(edge, "sec", sector_pairs(sectors, 0))
        edge_b = lax.ppermute(edge, "sec", sector_pairs(sectors, 1))
        sent = edge
    else:
        *packed, even, odd = pl.pallas_call(
            lambda *refs: pack_kernel(times, fields, held, *refs),
            out_shape=[
                pltpu.VMEM((held * fields + extra, 4, cells), f32) for extra in (4, 4, 4)
            ]
            + [pltpu.VMEM((tiles * 4 + (32 if held == times else 0), cells), f32)] * 2,
            in_specs=[VMEM, VMEM, SMEM, VMEM],
            out_specs=[VMEM] * 5,
            compiler_params=LIMIT,
            name="pack",
        )(swapped, edge, place, local)
        sent = packed[0]
        near = [
            lax.ppermute(block, "sec", [(k, k ^ distance) for k in range(sectors)])
            for distance, block in zip((1, 2, 3), packed)
        ]
        sources = [swapped] + near
        edge_a, edge_b = near[0][held * fields :], near[2][held * fields :]
    even = lax.ppermute(even, ("row", "span"), slab_pairs(slabs, 0))
    odd = lax.ppermute(odd, ("row", "span"), slab_pairs(slabs, 1))
    partial, mix = pl.pallas_call(
        lambda *refs: inner_kernel(times, fields, *refs),
        out_shape=[
            pltpu.VMEM((tiles * 16, cells), f32),
            pltpu.VMEM((2 * fields - 1, 8, cells), f32),
        ],
        in_specs=[VMEM, VMEM, SMEM, SMEM, ANY],
        out_specs=[VMEM, VMEM],
        compiler_params=LIMIT,
        cost_estimate=pl.CostEstimate(
            flops=tiles * 16 * cells * 50000, bytes_accessed=tiles * 16 * cells * 8000, transcendentals=0
        ),
        name="inner",
    )(local, coeff, jacobian, frequency, sent)
    total = pl.pallas_call(
        lambda *refs: sector_kernel(times, fields, *refs),
        out_shape=pltpu.VMEM((tiles * 16, cells), f32),
        in_specs=[VMEM, VMEM, SMEM] + [VMEM] * (3 + len(sources)),
        out_specs=VMEM,
        compiler_params=LIMIT,
        name="sectors",
    )(partial, mix, place, coeff, edge_a, edge_b, *sources)
    out, _ = pl.pallas_call(
        lambda *refs: finish_kernel(times, fields, *refs),
        out_shape=[pltpu.HBM((tiles * 16, cells), f32), pltpu.VMEM((tiles * 16, cells), f32)],
        in_specs=[VMEM] * 4,
        out_specs=[ANY, VMEM],
        scratch_shapes=[pltpu.SemaphoreType.DMA(((times + 1) // 2,))],
        input_output_aliases={0: 1},
        compiler_params=LIMIT,
        name="finish",
    )(total, coeff, even, odd)
    return out


def on_device(state, viscosity, jacobian, frequency, offsets):
    _, times, fields, axial, spans, cells = state.shape
    tiles = times * fields
    sectors, slabs = lax.axis_size("sec"), lax.axis_size("span")
    flat = state.reshape(tiles * 16, cells)
    coeff = viscosity.reshape(16, cells)
    f32 = jnp.float32
    swapped = lax.ppermute(flat, "row", [(0, 1), (1, 0)])
    local, edge, coeff, jac, place, size = pl.pallas_call(
        lambda *refs: collect_kernel(times, fields, *refs),
        out_shape=[
            pltpu.VMEM((tiles * 16, cells), f32),
            pltpu.VMEM((4, 4, cells), f32),
            pltpu.VMEM((16, cells), f32),
            pltpu.SMEM((fields, 1, fields), f32),
            pltpu.SMEM((8 * times,), jnp.int32),
            pltpu.SMEM((1,), jnp.int32),
        ],
        in_specs=[ANY] * 4,
        out_specs=[VMEM] * 3 + [SMEM] * 3,
        scratch_shapes=[
            pltpu.SMEM((times,), jnp.int32),
            pltpu.SemaphoreType.DMA((times,)),
            pltpu.SemaphoreType.DMA((3,)),
        ],
        compiler_params=LIMIT,
        name="collect",
    )(
        *(
            pltpu.with_memory_space_constraint(x, pltpu.HBM)
            for x in (flat, coeff, jnp.swapaxes(jacobian, 0, 1), offsets)
        )
    )
    operands = (swapped, local, edge, place, coeff, jac, frequency)
    if sectors == 4:
        branches = [
            lambda *held_operands, held=held: exchange(times, fields, held, *held_operands)
            for held in range((times + 1) // 2, times + 1)
        ]
        out = lax.switch(size[0], branches, *operands)
    else:
        out = exchange(times, fields, None, *operands)
    return out.reshape(state.shape)


def solution(mesh):
    return jax.shard_map(
        on_device,
        mesh=mesh,
        in_specs=(
            P("row", None, None, None, "span", "sec"),
            P("row", None, "span", "sec"),
            P("row", None, None),
            P("row"),
            P(),
        ),
        out_specs=P("row", None, None, None, "span", "sec"),
        check_vma=False,
    )
```

```python
import math

import jax
import jax.numpy as jnp
from jax import lax
from jax.experimental import pallas as pl
from jax.experimental.pallas import tpu as pltpu
from jax.sharding import PartitionSpec as P

VMEM = pl.BlockSpec(memory_space=pltpu.VMEM)
SMEM = pl.BlockSpec(memory_space=pltpu.SMEM)
ANY = pl.BlockSpec(memory_space=pl.ANY)
LIMIT = pltpu.CompilerParams(vmem_limit_bytes=32 * 1024 * 1024)


def sector_pairs(count, first):
    return [
        pair
        for low in range(first, count, 2)
        for pair in ((low, (low + 1) % count), ((low + 1) % count, low))
    ]


def slab_pairs(count, first):
    route = []
    for row in range(2):
        for here in range(count):
            there = here ^ 1 if first == 0 else ((here - 1) ^ 1) + 1
            if 0 <= there < count:
                route.append((row * count + here, row * count + there))
            else:
                route.append((row * count + here, (1 - row) * count + here))
    return route


def collect_kernel(
    times,
    fields,
    source_ref,
    coeff_source_ref,
    jac_source_ref,
    offset_source_ref,
    state_ref,
    edge_ref,
    coeff_ref,
    jac_ref,
    place_ref,
    size_ref,
    offset_ref,
    sems,
    small_sems,
):
    block_rows = fields * 16
    for n in range(8 * times):
        place_ref[n] = 0
    small = [
        pltpu.make_async_copy(source, target, small_sems.at[n])
        for n, (source, target) in enumerate(
            (
                (offset_source_ref, offset_ref),
                (coeff_source_ref, coeff_ref),
                (jac_source_ref, jac_ref),
            )
        )
    ]

    def piece(t):
        rows = pl.ds(t * block_rows, block_rows)
        return pltpu.make_async_copy(source_ref.at[rows, :], state_ref.at[rows, :], sems.at[t])

    for t in range(times):
        piece(t).start()
    for copy in small:
        copy.start()
    lane = lax.broadcasted_iota(jnp.int32, (16, 128), 1)
    edge = jnp.zeros((16, 128), jnp.float32)
    for t in range(times):
        piece(t).wait()
    for t in range(times):
        for f in range(fields):
            i = t * fields + f
            block = state_ref[pl.ds(16 * i, 16), :]
            here = jnp.logical_or(lane == 2 * i, lane == 2 * i + 1)
            edge = jnp.where(here, pltpu.roll(block, 2 * i + 1, 1), edge)
    for a in range(4):
        edge_ref[a] = edge[4 * a : 4 * a + 4]

    for copy in small:
        copy.wait()
    sectors = lax.axis_size("sec")
    row, sec = lax.axis_index("row"), lax.axis_index("sec")
    places = []
    for t in range(times):
        offset = offset_ref[t]
        cut = jnp.bitwise_and(offset, 127)
        whole = jnp.where(row == 0, offset >> 7, sectors - 1 - (offset >> 7))
        near = jnp.where(sec >= whole, sec - whole, sec - whole + sectors)
        far = jnp.where(near > 0, near - 1, sectors - 1)
        place_ref[5 * t + 4] = jnp.where(row == 0, cut, 128 - cut)
        if sectors != 4:
            place_ref[5 * t] = near
            place_ref[5 * t + 1] = t
            place_ref[5 * t + 2] = far
            place_ref[5 * t + 3] = t
        else:
            place_ref[5 * t] = near ^ sec
            place_ref[5 * t + 2] = far ^ sec
            places.append(whole)
    if sectors == 4:
        used = [jnp.int32(0)] * 4
        for t, whole in enumerate(places):
            after = (whole + 1) & 3
            near_place, far_place = jnp.int32(0), jnp.int32(0)
            for ahead in range(1, 4):
                near_place = jnp.where(whole == ahead, used[ahead], near_place)
                far_place = jnp.where(after == ahead, used[ahead], far_place)
                place_ref[(4 + ahead) * times + used[ahead]] = t
                wanted = jnp.logical_or(whole == ahead, after == ahead)
                used[ahead] = used[ahead] + wanted.astype(jnp.int32)
            place_ref[5 * t + 1] = near_place
            place_ref[5 * t + 3] = far_place
        largest = jnp.maximum(jnp.maximum(used[1], used[2]), used[3])
        size_ref[0] = largest - (times + 1) // 2
    else:
        size_ref[0] = 0


def span_kernel(state_ref, even_ref, odd_ref):
    slab, slabs = lax.axis_index("span"), lax.axis_size("span")
    parity = lax.rem(slab, 2)
    paired_even = (slab ^ 1) < slabs
    paired_odd = jnp.logical_and(slab > 0, ((slab - 1) ^ 1) + 1 < slabs)
    low = state_ref[pl.ds(0, state_ref.shape[0] // 4, stride=4), :]
    high = state_ref[pl.ds(3, state_ref.shape[0] // 4, stride=4), :]
    even_ref[: low.shape[0], :] = jnp.where(paired_even, jnp.where(parity == 0, high, low), 0.0)
    odd_ref[: low.shape[0], :] = jnp.where(paired_odd, jnp.where(parity == 0, low, high), 0.0)


def pack_kernel(
    times,
    fields,
    held,
    swapped_ref,
    edge_ref,
    place_ref,
    state_ref,
    x_ref,
    y_ref,
    d_ref,
    even_ref,
    odd_ref,
):
    even = lax.rem(lax.axis_index("sec"), 2) == 0
    for distance, packed_ref in ((1, x_ref), (2, y_ref), (3, d_ref)):
        ahead = jnp.int32(2)
        if distance != 2:
            ahead = jnp.where(even, distance, 4 - distance)
        for j in range(held):
            t = place_ref[(4 + ahead) * times + j]
            for f in range(fields):
                start = (t * fields + f) * 16 + 12
                packed_ref[j * fields + f] = swapped_ref[pl.ds(start, 4), :]
        if distance != 2:
            for a in range(4):
                packed_ref[held * fields + a] = edge_ref[a]
    span_kernel(state_ref, even_ref, odd_ref)


def inner_kernel(
    times,
    fields,
    state_ref,
    coeff_ref,
    jac_ref,
    omega_ref,
    _,
    partial_ref,
    mix_ref,
):
    lane = lax.broadcasted_iota(jnp.int32, (8, 128), 1)
    sub = lax.broadcasted_iota(jnp.int32, (8, 128), 0)
    lower = sub < 4
    bottom = sub % 4 == 0
    top = sub % 4 == 3
    coeff = [0.1 * coeff_ref[0:8, :], 0.1 * coeff_ref[8:16, :]]
    own = [0.8 - 4.0 * c for c in coeff]
    rate = -0.1 * omega_ref[0]
    weight = [0.0]
    weight += [0.5 * (-1.0) ** m / math.sin(math.pi * m / times) for m in range(1, times)]

    field = (lane // 2) % fields
    sign = jnp.where(lane % 2 == 0, -0.05, 0.05)
    for distance in range(1 - fields, fields):
        mix = jnp.zeros((8, 128), jnp.float32)
        for f in range(max(0, distance), min(fields, fields + distance)):
            mix = jnp.where(field == f, jac_ref[f, 0, f - distance], mix)
        mix_ref[fields - 1 + distance] = sign * mix

    def step(t, _):
        def load(u, f, h):
            start = pl.multiple_of((u * fields + f) * 16 + 8 * h, 8)
            return state_ref[pl.ds(start, 8), :]

        difference, result = [], []
        for f in range(fields):
            v0, v1 = load(t, f, 0), load(t, f, 1)
            r0, r1 = pltpu.roll(v0, 4, 0), pltpu.roll(v1, 4, 0)
            middle = jnp.where(lower, r0, r1)
            axial = [middle + jnp.where(lower, 0.0, r0), jnp.where(lower, r1, 0.0) + middle]
            differences, results = [], []
            for h, v in enumerate((v0, v1)):
                plus = jnp.where(lane == 127, 0.0, pltpu.roll(v, 127, 1))
                minus = jnp.where(lane == 0, 0.0, pltpu.roll(v, 1, 1))
                up = jnp.where(top, 0.0, pltpu.roll(v, 7, 0))
                down = jnp.where(bottom, 0.0, pltpu.roll(v, 1, 0))
                differences.append(plus - minus)
                value = own[h] * v + coeff[h] * ((plus + minus) + (up + down)) + 0.1 * axial[h]
                spectral = jnp.zeros_like(v)
                for m in range(1, times // 2 + 1):
                    before = load(lax.rem(t + times - m, times), f, h)
                    after = load(lax.rem(t + m, times), f, h)
                    spectral = spectral + weight[m] * (before - after)
                results.append(value + rate * spectral)
            difference.append(differences)
            result.append(results)
        for f in range(fields):
            for h in range(2):
                value = result[f][h]
                for g in range(fields):
                    value = value + (-0.05 * jac_ref[f, 0, g]) * difference[g][h]
                start = pl.multiple_of((t * fields + f) * 16 + 8 * h, 8)
                partial_ref[pl.ds(start, 8), :] = value
        return 0

    lax.fori_loop(0, times, step, 0)


def edge_terms(fields, mix_ref, coeff_ref, edge_a_ref, edge_b_ref):
    even = lax.rem(lax.axis_index("sec"), 2) == 0
    sides = lax.broadcasted_iota(jnp.int32, (8, 128), 1) % 2 == 0
    terms = []
    for h in range(2):
        edge_a = jnp.concatenate([edge_a_ref[2 * h], edge_a_ref[2 * h + 1]], axis=0)
        edge_b = jnp.concatenate([edge_b_ref[2 * h], edge_b_ref[2 * h + 1]], axis=0)
        plus_edge = jnp.where(even, edge_a, edge_b)
        minus_edge = jnp.where(even, edge_b, edge_a)
        halo = jnp.where(sides, pltpu.roll(plus_edge, 127, 1), pltpu.roll(minus_edge, 1, 1))
        coeff = 0.1 * coeff_ref[8 * h : 8 * h + 8, :]
        term = jnp.where(sides, coeff[:, 127:128], coeff[:, 0:1]) * halo
        for distance in range(1 - fields, fields):
            term = term + mix_ref[fields - 1 + distance] * pltpu.roll(halo, (2 * distance) % 128, 1)
        terms.append(term)
    return terms


def sector_kernel(
    times, fields, partial_ref, mix_ref, place_ref, coeff_ref, edge_a_ref, edge_b_ref, *rest
):
    source_refs, total_ref = rest[:-1], rest[-1]
    lane = lax.broadcasted_iota(jnp.int32, (8, 128), 1)
    lower = lax.broadcasted_iota(jnp.int32, (8, 128), 0) < 4
    lane4 = lax.broadcasted_iota(jnp.int32, (4, 128), 1)
    outside = jnp.logical_or(lane == 0, lane == 127)
    edges = edge_terms(fields, mix_ref, coeff_ref, edge_a_ref, edge_b_ref)

    def pick(slot, place, t, f):
        if len(source_refs) == 1:
            return source_refs[0][slot, pl.ds((place * fields + f) * 4, 4), :]
        value = source_refs[0][pl.ds((t * fields + f) * 16 + 12, 4), :]
        for other in range(1, 4):
            value = jnp.where(slot == other, source_refs[other][place * fields + f], value)
        return value

    def step(t, _):
        near, near_place, far, far_place, part = [place_ref[5 * t + n] for n in range(5)]
        for f in range(fields):
            index = t * fields + f
            ghost = jnp.where(
                lane4 >= 128 - part, pick(far, far_place, t, f), pick(near, near_place, t, f)
            )
            ghost = pltpu.roll(ghost, jnp.bitwise_and(part, 127), 1)
            ghost = jnp.concatenate([ghost, ghost], axis=0)
            for h in range(2):
                rows = pl.ds(pl.multiple_of(index * 16 + 8 * h, 8), 8)
                value = partial_ref[rows, :]
                value = value + jnp.where(outside, pltpu.roll(edges[h], 127 - 2 * index, 1), 0.0)
                if h == 1:
                    value = value + jnp.where(lower, 0.0, 0.1 * ghost)
                total_ref[rows, :] = value
        return 0

    lax.fori_loop(0, times, step, 0, unroll=9)


def finish_kernel(
    times, fields, total_ref, coeff_ref, even_ref, odd_ref, out_ref, result_ref, sems
):
    straight = lax.rem(lax.axis_index("span"), 2) == 0
    coeff = []
    for s in (0, 3):
        four = 0.1 * coeff_ref[pl.ds(s, 4, stride=4), :]
        coeff.append(jnp.concatenate([four, four], axis=0))

    def piece(n, first, last):
        rows = pl.ds(first * fields * 16, (last - first) * fields * 16)
        return pltpu.make_async_copy(result_ref.at[rows, :], out_ref.at[rows, :], sems.at[n])

    pieces = [(first, min(first + 2, times)) for first in range(0, times, 2)]
    for n, (first, last) in enumerate(pieces):
        low, high = first * fields * 4, last * fields * 4
        for start in range(low, high, 8):
            size = min(8, high - start)
            even, odd = even_ref[start : start + size, :], odd_ref[start : start + size, :]
            halos = jnp.where(straight, odd, even), jnp.where(straight, even, odd)
            for s, halo, factor in zip((0, 3), halos, coeff):
                rows = pl.ds(4 * start + s, size, stride=4)
                result_ref[rows, :] = total_ref[rows, :] + factor[:size] * halo
        piece(n, first, last).start()
    for n, (first, last) in enumerate(pieces):
        piece(n, first, last).wait()


def exchange(times, fields, held, swapped, local, edge, place, coeff, jacobian, frequency):
    f32 = jnp.float32
    tiles, cells = times * fields, local.shape[1]
    sectors, slabs = lax.axis_size("sec"), lax.axis_size("span")
    if held is None:
        even, odd = pl.pallas_call(
            span_kernel,
            out_shape=[pltpu.VMEM((tiles * 4, cells), f32)] * 2,
            in_specs=[VMEM],
            out_specs=[VMEM] * 2,
            compiler_params=LIMIT,
            name="spans",
        )(local)
        strip = swapped.reshape(tiles, 16, cells)[:, 12:].reshape(tiles * 4, cells)
        sources = [lax.all_gather(strip, "sec")]
        edge_a = lax.ppermute(edge, "sec", sector_pairs(sectors, 0))
        edge_b = lax.ppermute(edge, "sec", sector_pairs(sectors, 1))
        sent = edge
    else:
        *packed, even, odd = pl.pallas_call(
            lambda *refs: pack_kernel(times, fields, held, *refs),
            out_shape=[
                pltpu.VMEM((held * fields + extra, 4, cells), f32) for extra in (4, 4, 4)
            ]
            + [pltpu.VMEM((tiles * 4 + (32 if held == times else 0), cells), f32)] * 2,
            in_specs=[VMEM, VMEM, SMEM, VMEM],
            out_specs=[VMEM] * 5,
            compiler_params=LIMIT,
            name="pack",
        )(swapped, edge, place, local)
        sent = packed[0]
        near = [
            lax.ppermute(block, "sec", [(k, k ^ distance) for k in range(sectors)])
            for distance, block in zip((1, 2, 3), packed)
        ]
        sources = [swapped] + near
        edge_a, edge_b = near[0][held * fields :], near[2][held * fields :]
    even = lax.ppermute(even, ("row", "span"), slab_pairs(slabs, 0))
    odd = lax.ppermute(odd, ("row", "span"), slab_pairs(slabs, 1))
    partial, mix = pl.pallas_call(
        lambda *refs: inner_kernel(times, fields, *refs),
        out_shape=[
            pltpu.VMEM((tiles * 16, cells), f32),
            pltpu.VMEM((2 * fields - 1, 8, cells), f32),
        ],
        in_specs=[VMEM, VMEM, SMEM, SMEM, ANY],
        out_specs=[VMEM, VMEM],
        compiler_params=LIMIT,
        cost_estimate=pl.CostEstimate(
            flops=tiles * 16 * cells * 50000, bytes_accessed=tiles * 16 * cells * 8000, transcendentals=0
        ),
        name="inner",
    )(local, coeff, jacobian, frequency, sent)
    total = pl.pallas_call(
        lambda *refs: sector_kernel(times, fields, *refs),
        out_shape=pltpu.VMEM((tiles * 16, cells), f32),
        in_specs=[VMEM, VMEM, SMEM] + [VMEM] * (3 + len(sources)),
        out_specs=VMEM,
        compiler_params=LIMIT,
        name="sectors",
    )(partial, mix, place, coeff, edge_a, edge_b, *sources)
    out, _ = pl.pallas_call(
        lambda *refs: finish_kernel(times, fields, *refs),
        out_shape=[pltpu.HBM((tiles * 16, cells), f32), pltpu.VMEM((tiles * 16, cells), f32)],
        in_specs=[VMEM] * 4,
        out_specs=[ANY, VMEM],
        scratch_shapes=[pltpu.SemaphoreType.DMA(((times + 1) // 2,))],
        input_output_aliases={0: 1},
        compiler_params=LIMIT,
        name="finish",
    )(total, coeff, even, odd)
    return out


def on_device(state, viscosity, jacobian, frequency, offsets):
    _, times, fields, axial, spans, cells = state.shape
    tiles = times * fields
    sectors, slabs = lax.axis_size("sec"), lax.axis_size("span")
    flat = state.reshape(tiles * 16, cells)
    coeff = viscosity.reshape(16, cells)
    f32 = jnp.float32
    swapped = lax.ppermute(flat, "row", [(0, 1), (1, 0)])
    local, edge, coeff, jac, place, size = pl.pallas_call(
        lambda *refs: collect_kernel(times, fields, *refs),
        out_shape=[
            pltpu.VMEM((tiles * 16, cells), f32),
            pltpu.VMEM((4, 4, cells), f32),
            pltpu.VMEM((16, cells), f32),
            pltpu.SMEM((fields, 1, fields), f32),
            pltpu.SMEM((8 * times,), jnp.int32),
            pltpu.SMEM((1,), jnp.int32),
        ],
        in_specs=[ANY] * 4,
        out_specs=[VMEM] * 3 + [SMEM] * 3,
        scratch_shapes=[
            pltpu.SMEM((times,), jnp.int32),
            pltpu.SemaphoreType.DMA((times,)),
            pltpu.SemaphoreType.DMA((3,)),
        ],
        compiler_params=LIMIT,
        name="collect",
    )(
        *(
            pltpu.with_memory_space_constraint(x, pltpu.HBM)
            for x in (flat, coeff, jnp.swapaxes(jacobian, 0, 1), offsets)
        )
    )
    operands = (swapped, local, edge, place, coeff, jac, frequency)
    if sectors == 4:
        branches = [
            lambda *held_operands, held=held: exchange(times, fields, held, *held_operands)
            for held in range((times + 1) // 2, times + 1)
        ]
        out = lax.switch(size[0], branches, *operands)
    else:
        out = exchange(times, fields, None, *operands)
    return out.reshape(state.shape)


def solution(mesh):
    return jax.shard_map(
        on_device,
        mesh=mesh,
        in_specs=(
            P("row", None, None, None, "span", "sec"),
            P("row", None, "span", "sec"),
            P("row", None, None),
            P("row"),
            P(),
        ),
        out_specs=P("row", None, None, None, "span", "sec"),
        check_vma=False,
    )
```

```python
import math

import jax
import jax.numpy as jnp
from jax import lax
from jax.experimental import pallas as pl
from jax.experimental.pallas import tpu as pltpu
from jax.sharding import PartitionSpec as P

VMEM = pl.BlockSpec(memory_space=pltpu.VMEM)
SMEM = pl.BlockSpec(memory_space=pltpu.SMEM)
ANY = pl.BlockSpec(memory_space=pl.ANY)
LIMIT = pltpu.CompilerParams(vmem_limit_bytes=32 * 1024 * 1024)


def sector_pairs(count, first):
    return [
        pair
        for low in range(first, count, 2)
        for pair in ((low, (low + 1) % count), ((low + 1) % count, low))
    ]


def slab_pairs(count, first):
    route = []
    for row in range(2):
        for here in range(count):
            there = here ^ 1 if first == 0 else ((here - 1) ^ 1) + 1
            paired = 0 <= there < count
            swap = crosses(first, there > here) if paired else True
            target = there if paired else here
            route.append((row * count + here, (1 - row if swap else row) * count + target))
    return route


def crosses(first, upward):
    return first == 1 or upward


def collect_kernel(
    times,
    fields,
    source_ref,
    coeff_source_ref,
    jac_source_ref,
    offset_source_ref,
    state_ref,
    edge_ref,
    coeff_ref,
    jac_ref,
    place_ref,
    size_ref,
    offset_ref,
    sems,
    small_sems,
):
    block_rows = fields * 16
    for n in range(8 * times):
        place_ref[n] = 0
    small = [
        pltpu.make_async_copy(source, target, small_sems.at[n])
        for n, (source, target) in enumerate(
            (
                (offset_source_ref, offset_ref),
                (coeff_source_ref, coeff_ref),
                (jac_source_ref, jac_ref),
            )
        )
    ]

    def piece(t):
        rows = pl.ds(t * block_rows, block_rows)
        return pltpu.make_async_copy(source_ref.at[rows, :], state_ref.at[rows, :], sems.at[t])

    for t in range(times):
        piece(t).start()
    for copy in small:
        copy.start()
    lane = lax.broadcasted_iota(jnp.int32, (16, 128), 1)
    edge = jnp.zeros((16, 128), jnp.float32)
    for t in range(times):
        piece(t).wait()
    for t in range(times):
        for f in range(fields):
            i = t * fields + f
            block = state_ref[pl.ds(16 * i, 16), :]
            here = jnp.logical_or(lane == 2 * i, lane == 2 * i + 1)
            edge = jnp.where(here, pltpu.roll(block, 2 * i + 1, 1), edge)
    for a in range(4):
        edge_ref[a] = edge[4 * a : 4 * a + 4]

    for copy in small:
        copy.wait()
    sectors = lax.axis_size("sec")
    row, sec = lax.axis_index("row"), lax.axis_index("sec")
    places = []
    for t in range(times):
        offset = offset_ref[t]
        cut = jnp.bitwise_and(offset, 127)
        whole = jnp.where(row == 0, offset >> 7, sectors - 1 - (offset >> 7))
        near = jnp.where(sec >= whole, sec - whole, sec - whole + sectors)
        far = jnp.where(near > 0, near - 1, sectors - 1)
        place_ref[5 * t + 4] = jnp.where(row == 0, cut, 128 - cut)
        if sectors != 4:
            place_ref[5 * t] = near
            place_ref[5 * t + 1] = t
            place_ref[5 * t + 2] = far
            place_ref[5 * t + 3] = t
        else:
            place_ref[5 * t] = near ^ sec
            place_ref[5 * t + 2] = far ^ sec
            places.append(whole)
    if sectors == 4:
        used = [jnp.int32(0)] * 4
        for t, whole in enumerate(places):
            after = (whole + 1) & 3
            near_place, far_place = jnp.int32(0), jnp.int32(0)
            for ahead in range(1, 4):
                near_place = jnp.where(whole == ahead, used[ahead], near_place)
                far_place = jnp.where(after == ahead, used[ahead], far_place)
                place_ref[(4 + ahead) * times + used[ahead]] = t
                wanted = jnp.logical_or(whole == ahead, after == ahead)
                used[ahead] = used[ahead] + wanted.astype(jnp.int32)
            place_ref[5 * t + 1] = near_place
            place_ref[5 * t + 3] = far_place
        largest = jnp.maximum(jnp.maximum(used[1], used[2]), used[3])
        size_ref[0] = largest - (times + 1) // 2
    else:
        size_ref[0] = 0


def span_kernel(state_ref, swapped_ref, even_ref, odd_ref):
    slab, slabs = lax.axis_index("span"), lax.axis_size("span")
    upward = lax.rem(slab, 2) == 0
    rows = state_ref.shape[0] // 4
    for first, target_ref in ((0, even_ref), (1, odd_ref)):
        paired = (slab ^ 1) < slabs
        if first == 1:
            paired = jnp.logical_and(slab > 0, ((slab - 1) ^ 1) + 1 < slabs)
        top = upward if first == 0 else jnp.logical_not(upward)
        swap = crosses(first, top)

        def fill(ref, target_ref=target_ref, top=top, paired=paired):
            low = ref[pl.ds(0, rows, stride=4), :]
            high = ref[pl.ds(3, rows, stride=4), :]
            target_ref[:rows, :] = jnp.where(paired, jnp.where(top, high, low), 0.0)

        if isinstance(swap, bool):
            fill(swapped_ref if swap else state_ref)
        else:
            pl.when(swap)(lambda fill=fill: fill(swapped_ref))
            pl.when(jnp.logical_not(swap))(lambda fill=fill: fill(state_ref))


def pack_kernel(
    times,
    fields,
    held,
    swapped_ref,
    edge_ref,
    place_ref,
    state_ref,
    x_ref,
    y_ref,
    d_ref,
    even_ref,
    odd_ref,
):
    even = lax.rem(lax.axis_index("sec"), 2) == 0
    for distance, packed_ref in ((1, x_ref), (2, y_ref), (3, d_ref)):
        ahead = jnp.int32(2)
        if distance != 2:
            ahead = jnp.where(even, distance, 4 - distance)
        for j in range(held):
            t = place_ref[(4 + ahead) * times + j]
            for f in range(fields):
                start = (t * fields + f) * 16 + 12
                packed_ref[j * fields + f] = swapped_ref[pl.ds(start, 4), :]
        if distance != 2:
            for a in range(4):
                packed_ref[held * fields + a] = edge_ref[a]
    span_kernel(state_ref, swapped_ref, even_ref, odd_ref)


def inner_kernel(
    times,
    fields,
    state_ref,
    coeff_ref,
    jac_ref,
    omega_ref,
    _,
    partial_ref,
    mix_ref,
):
    lane = lax.broadcasted_iota(jnp.int32, (8, 128), 1)
    sub = lax.broadcasted_iota(jnp.int32, (8, 128), 0)
    lower = sub < 4
    bottom = sub % 4 == 0
    top = sub % 4 == 3
    coeff = [0.1 * coeff_ref[0:8, :], 0.1 * coeff_ref[8:16, :]]
    own = [0.8 - 4.0 * c for c in coeff]
    rate = -0.1 * omega_ref[0]
    weight = [0.0]
    weight += [0.5 * (-1.0) ** m / math.sin(math.pi * m / times) for m in range(1, times)]

    field = (lane // 2) % fields
    sign = jnp.where(lane % 2 == 0, -0.05, 0.05)
    for distance in range(1 - fields, fields):
        mix = jnp.zeros((8, 128), jnp.float32)
        for f in range(max(0, distance), min(fields, fields + distance)):
            mix = jnp.where(field == f, jac_ref[f, 0, f - distance], mix)
        mix_ref[fields - 1 + distance] = sign * mix

    def step(t, _):
        def load(u, f, h):
            start = pl.multiple_of((u * fields + f) * 16 + 8 * h, 8)
            return state_ref[pl.ds(start, 8), :]

        difference, result = [], []
        for f in range(fields):
            v0, v1 = load(t, f, 0), load(t, f, 1)
            r0, r1 = pltpu.roll(v0, 4, 0), pltpu.roll(v1, 4, 0)
            middle = jnp.where(lower, r0, r1)
            axial = [middle + jnp.where(lower, 0.0, r0), jnp.where(lower, r1, 0.0) + middle]
            differences, results = [], []
            for h, v in enumerate((v0, v1)):
                plus = jnp.where(lane == 127, 0.0, pltpu.roll(v, 127, 1))
                minus = jnp.where(lane == 0, 0.0, pltpu.roll(v, 1, 1))
                up = jnp.where(top, 0.0, pltpu.roll(v, 7, 0))
                down = jnp.where(bottom, 0.0, pltpu.roll(v, 1, 0))
                differences.append(plus - minus)
                value = own[h] * v + coeff[h] * ((plus + minus) + (up + down)) + 0.1 * axial[h]
                spectral = jnp.zeros_like(v)
                for m in range(1, times // 2 + 1):
                    before = load(lax.rem(t + times - m, times), f, h)
                    after = load(lax.rem(t + m, times), f, h)
                    spectral = spectral + weight[m] * (before - after)
                results.append(value + rate * spectral)
            difference.append(differences)
            result.append(results)
        for f in range(fields):
            for h in range(2):
                value = result[f][h]
                for g in range(fields):
                    value = value + (-0.05 * jac_ref[f, 0, g]) * difference[g][h]
                start = pl.multiple_of((t * fields + f) * 16 + 8 * h, 8)
                partial_ref[pl.ds(start, 8), :] = value
        return 0

    lax.fori_loop(0, times, step, 0)


def edge_terms(fields, mix_ref, coeff_ref, edge_a_ref, edge_b_ref):
    even = lax.rem(lax.axis_index("sec"), 2) == 0
    sides = lax.broadcasted_iota(jnp.int32, (8, 128), 1) % 2 == 0
    terms = []
    for h in range(2):
        edge_a = jnp.concatenate([edge_a_ref[2 * h], edge_a_ref[2 * h + 1]], axis=0)
        edge_b = jnp.concatenate([edge_b_ref[2 * h], edge_b_ref[2 * h + 1]], axis=0)
        plus_edge = jnp.where(even, edge_a, edge_b)
        minus_edge = jnp.where(even, edge_b, edge_a)
        halo = jnp.where(sides, pltpu.roll(plus_edge, 127, 1), pltpu.roll(minus_edge, 1, 1))
        coeff = 0.1 * coeff_ref[8 * h : 8 * h + 8, :]
        term = jnp.where(sides, coeff[:, 127:128], coeff[:, 0:1]) * halo
        for distance in range(1 - fields, fields):
            term = term + mix_ref[fields - 1 + distance] * pltpu.roll(halo, (2 * distance) % 128, 1)
        terms.append(term)
    return terms


def sector_kernel(
    times, fields, partial_ref, mix_ref, place_ref, coeff_ref, edge_a_ref, edge_b_ref, *rest
):
    source_refs, total_ref = rest[:-1], rest[-1]
    lane = lax.broadcasted_iota(jnp.int32, (8, 128), 1)
    lower = lax.broadcasted_iota(jnp.int32, (8, 128), 0) < 4
    lane4 = lax.broadcasted_iota(jnp.int32, (4, 128), 1)
    outside = jnp.logical_or(lane == 0, lane == 127)
    edges = edge_terms(fields, mix_ref, coeff_ref, edge_a_ref, edge_b_ref)

    def pick(slot, place, t, f):
        if len(source_refs) == 1:
            return source_refs[0][slot, pl.ds((place * fields + f) * 4, 4), :]
        value = source_refs[0][pl.ds((t * fields + f) * 16 + 12, 4), :]
        for other in range(1, 4):
            value = jnp.where(slot == other, source_refs[other][place * fields + f], value)
        return value

    def step(t, _):
        near, near_place, far, far_place, part = [place_ref[5 * t + n] for n in range(5)]
        for f in range(fields):
            index = t * fields + f
            ghost = jnp.where(
                lane4 >= 128 - part, pick(far, far_place, t, f), pick(near, near_place, t, f)
            )
            ghost = pltpu.roll(ghost, jnp.bitwise_and(part, 127), 1)
            ghost = jnp.concatenate([ghost, ghost], axis=0)
            for h in range(2):
                rows = pl.ds(pl.multiple_of(index * 16 + 8 * h, 8), 8)
                value = partial_ref[rows, :]
                value = value + jnp.where(outside, pltpu.roll(edges[h], 127 - 2 * index, 1), 0.0)
                if h == 1:
                    value = value + jnp.where(lower, 0.0, 0.1 * ghost)
                total_ref[rows, :] = value
        return 0

    lax.fori_loop(0, times, step, 0, unroll=9)


def finish_kernel(
    times, fields, total_ref, coeff_ref, even_ref, odd_ref, out_ref, result_ref, sems
):
    straight = lax.rem(lax.axis_index("span"), 2) == 0
    coeff = []
    for s in (0, 3):
        four = 0.1 * coeff_ref[pl.ds(s, 4, stride=4), :]
        coeff.append(jnp.concatenate([four, four], axis=0))

    def piece(n, first, last):
        rows = pl.ds(first * fields * 16, (last - first) * fields * 16)
        return pltpu.make_async_copy(result_ref.at[rows, :], out_ref.at[rows, :], sems.at[n])

    pieces = [(first, min(first + 2, times)) for first in range(0, times, 2)]
    for n, (first, last) in enumerate(pieces):
        low, high = first * fields * 4, last * fields * 4
        for start in range(low, high, 8):
            size = min(8, high - start)
            even, odd = even_ref[start : start + size, :], odd_ref[start : start + size, :]
            halos = jnp.where(straight, odd, even), jnp.where(straight, even, odd)
            for s, halo, factor in zip((0, 3), halos, coeff):
                rows = pl.ds(4 * start + s, size, stride=4)
                result_ref[rows, :] = total_ref[rows, :] + factor[:size] * halo
        piece(n, first, last).start()
    for n, (first, last) in enumerate(pieces):
        piece(n, first, last).wait()


def exchange(times, fields, held, swapped, local, edge, place, coeff, jacobian, frequency):
    f32 = jnp.float32
    tiles, cells = times * fields, local.shape[1]
    sectors, slabs = lax.axis_size("sec"), lax.axis_size("span")
    if held is None:
        even, odd = pl.pallas_call(
            span_kernel,
            out_shape=[pltpu.VMEM((tiles * 4, cells), f32)] * 2,
            in_specs=[VMEM] * 2,
            out_specs=[VMEM] * 2,
            compiler_params=LIMIT,
            name="spans",
        )(local, swapped)
        strip = swapped.reshape(tiles, 16, cells)[:, 12:].reshape(tiles * 4, cells)
        sources = [lax.all_gather(strip, "sec")]
        edge_a = lax.ppermute(edge, "sec", sector_pairs(sectors, 0))
        edge_b = lax.ppermute(edge, "sec", sector_pairs(sectors, 1))
        sent = edge
    else:
        *packed, even, odd = pl.pallas_call(
            lambda *refs: pack_kernel(times, fields, held, *refs),
            out_shape=[
                pltpu.VMEM((held * fields + extra, 4, cells), f32) for extra in (4, 4, 4)
            ]
            + [pltpu.VMEM((tiles * 4 + (32 if held == times else 0), cells), f32)] * 2,
            in_specs=[VMEM, VMEM, SMEM, VMEM],
            out_specs=[VMEM] * 5,
            compiler_params=LIMIT,
            name="pack",
        )(swapped, edge, place, local)
        sent = packed[0]
        near = [
            lax.ppermute(block, "sec", [(k, k ^ distance) for k in range(sectors)])
            for distance, block in zip((1, 2, 3), packed)
        ]
        sources = [swapped] + near
        edge_a, edge_b = near[0][held * fields :], near[2][held * fields :]
    even = lax.ppermute(even, ("row", "span"), slab_pairs(slabs, 0))
    odd = lax.ppermute(odd, ("row", "span"), slab_pairs(slabs, 1))
    partial, mix = pl.pallas_call(
        lambda *refs: inner_kernel(times, fields, *refs),
        out_shape=[
            pltpu.VMEM((tiles * 16, cells), f32),
            pltpu.VMEM((2 * fields - 1, 8, cells), f32),
        ],
        in_specs=[VMEM, VMEM, SMEM, SMEM, ANY],
        out_specs=[VMEM, VMEM],
        compiler_params=LIMIT,
        cost_estimate=pl.CostEstimate(
            flops=tiles * 16 * cells * 50000, bytes_accessed=tiles * 16 * cells * 8000, transcendentals=0
        ),
        name="inner",
    )(local, coeff, jacobian, frequency, sent)
    total = pl.pallas_call(
        lambda *refs: sector_kernel(times, fields, *refs),
        out_shape=pltpu.VMEM((tiles * 16, cells), f32),
        in_specs=[VMEM, VMEM, SMEM] + [VMEM] * (3 + len(sources)),
        out_specs=VMEM,
        compiler_params=LIMIT,
        name="sectors",
    )(partial, mix, place, coeff, edge_a, edge_b, *sources)
    out, _ = pl.pallas_call(
        lambda *refs: finish_kernel(times, fields, *refs),
        out_shape=[pltpu.HBM((tiles * 16, cells), f32), pltpu.VMEM((tiles * 16, cells), f32)],
        in_specs=[VMEM] * 4,
        out_specs=[ANY, VMEM],
        scratch_shapes=[pltpu.SemaphoreType.DMA(((times + 1) // 2,))],
        input_output_aliases={0: 1},
        compiler_params=LIMIT,
        name="finish",
    )(total, coeff, even, odd)
    return out


def on_device(state, viscosity, jacobian, frequency, offsets):
    _, times, fields, axial, spans, cells = state.shape
    tiles = times * fields
    sectors, slabs = lax.axis_size("sec"), lax.axis_size("span")
    flat = state.reshape(tiles * 16, cells)
    coeff = viscosity.reshape(16, cells)
    f32 = jnp.float32
    swapped = lax.ppermute(flat, "row", [(0, 1), (1, 0)])
    local, edge, coeff, jac, place, size = pl.pallas_call(
        lambda *refs: collect_kernel(times, fields, *refs),
        out_shape=[
            pltpu.VMEM((tiles * 16, cells), f32),
            pltpu.VMEM((4, 4, cells), f32),
            pltpu.VMEM((16, cells), f32),
            pltpu.SMEM((fields, 1, fields), f32),
            pltpu.SMEM((8 * times,), jnp.int32),
            pltpu.SMEM((1,), jnp.int32),
        ],
        in_specs=[ANY] * 4,
        out_specs=[VMEM] * 3 + [SMEM] * 3,
        scratch_shapes=[
            pltpu.SMEM((times,), jnp.int32),
            pltpu.SemaphoreType.DMA((times,)),
            pltpu.SemaphoreType.DMA((3,)),
        ],
        compiler_params=LIMIT,
        name="collect",
    )(
        *(
            pltpu.with_memory_space_constraint(x, pltpu.HBM)
            for x in (flat, coeff, jnp.swapaxes(jacobian, 0, 1), offsets)
        )
    )
    operands = (swapped, local, edge, place, coeff, jac, frequency)
    if sectors == 4:
        branches = [
            lambda *held_operands, held=held: exchange(times, fields, held, *held_operands)
            for held in range((times + 1) // 2, times + 1)
        ]
        out = lax.switch(size[0], branches, *operands)
    else:
        out = exchange(times, fields, None, *operands)
    return out.reshape(state.shape)


def solution(mesh):
    return jax.shard_map(
        on_device,
        mesh=mesh,
        in_specs=(
            P("row", None, None, None, "span", "sec"),
            P("row", None, "span", "sec"),
            P("row", None, None),
            P("row"),
            P(),
        ),
        out_specs=P("row", None, None, None, "span", "sec"),
        check_vma=False,
    )
```

```python
import math

import jax
import jax.numpy as jnp
from jax import lax
from jax.experimental import pallas as pl
from jax.experimental.pallas import tpu as pltpu
from jax.sharding import PartitionSpec as P

VMEM = pl.BlockSpec(memory_space=pltpu.VMEM)
SMEM = pl.BlockSpec(memory_space=pltpu.SMEM)
ANY = pl.BlockSpec(memory_space=pl.ANY)
LIMIT = pltpu.CompilerParams(vmem_limit_bytes=32 * 1024 * 1024)


def sector_pairs(count, first):
    return [
        pair
        for low in range(first, count, 2)
        for pair in ((low, (low + 1) % count), ((low + 1) % count, low))
    ]


def slab_pairs(count, first):
    route = []
    for row in range(2):
        for here in range(count):
            there = here ^ 1 if first == 0 else ((here - 1) ^ 1) + 1
            paired = 0 <= there < count
            swap = crosses(first, there > here) if paired else True
            target = there if paired else here
            route.append((row * count + here, (1 - row if swap else row) * count + target))
    return route


def crosses(first, upward):
    return first == 1 or upward


def collect_kernel(
    times,
    fields,
    source_ref,
    coeff_source_ref,
    jac_source_ref,
    offset_source_ref,
    state_ref,
    edge_ref,
    coeff_ref,
    jac_ref,
    place_ref,
    size_ref,
    offset_ref,
    sems,
    small_sems,
):
    block_rows = fields * 16
    for n in range(8 * times):
        place_ref[n] = 0
    small = [
        pltpu.make_async_copy(source, target, small_sems.at[n])
        for n, (source, target) in enumerate(
            (
                (offset_source_ref, offset_ref),
                (coeff_source_ref, coeff_ref),
                (jac_source_ref, jac_ref),
            )
        )
    ]

    def piece(t):
        rows = pl.ds(t * block_rows, block_rows)
        return pltpu.make_async_copy(source_ref.at[rows, :], state_ref.at[rows, :], sems.at[t])

    for t in range(times):
        piece(t).start()
    for copy in small:
        copy.start()
    lane = lax.broadcasted_iota(jnp.int32, (16, 128), 1)
    edge = jnp.zeros((16, 128), jnp.float32)
    for t in range(times):
        piece(t).wait()
    for t in range(times):
        for f in range(fields):
            i = t * fields + f
            block = state_ref[pl.ds(16 * i, 16), :]
            here = jnp.logical_or(lane == 2 * i, lane == 2 * i + 1)
            edge = jnp.where(here, pltpu.roll(block, 2 * i + 1, 1), edge)
    for a in range(4):
        edge_ref[a] = edge[4 * a : 4 * a + 4]

    for copy in small:
        copy.wait()
    sectors = lax.axis_size("sec")
    row, sec = lax.axis_index("row"), lax.axis_index("sec")
    places = []
    for t in range(times):
        offset = offset_ref[t]
        cut = jnp.bitwise_and(offset, 127)
        whole = jnp.where(row == 0, offset >> 7, sectors - 1 - (offset >> 7))
        near = jnp.where(sec >= whole, sec - whole, sec - whole + sectors)
        far = jnp.where(near > 0, near - 1, sectors - 1)
        place_ref[5 * t + 4] = jnp.where(row == 0, cut, 128 - cut)
        if sectors != 4:
            place_ref[5 * t] = near
            place_ref[5 * t + 1] = t
            place_ref[5 * t + 2] = far
            place_ref[5 * t + 3] = t
        else:
            place_ref[5 * t] = near ^ sec
            place_ref[5 * t + 2] = far ^ sec
            places.append(whole)
    if sectors == 4:
        used = [jnp.int32(0)] * 4
        for t, whole in enumerate(places):
            after = (whole + 1) & 3
            near_place, far_place = jnp.int32(0), jnp.int32(0)
            for ahead in range(1, 4):
                near_place = jnp.where(whole == ahead, used[ahead], near_place)
                far_place = jnp.where(after == ahead, used[ahead], far_place)
                place_ref[(4 + ahead) * times + used[ahead]] = t
                wanted = jnp.logical_or(whole == ahead, after == ahead)
                used[ahead] = used[ahead] + wanted.astype(jnp.int32)
            place_ref[5 * t + 1] = near_place
            place_ref[5 * t + 3] = far_place
        largest = jnp.maximum(jnp.maximum(used[1], used[2]), used[3])
        size_ref[0] = largest - (times + 1) // 2
    else:
        size_ref[0] = 0


def span_kernel(state_ref, swapped_ref, even_ref, odd_ref):
    slab, slabs = lax.axis_index("span"), lax.axis_size("span")
    upward = lax.rem(slab, 2) == 0
    rows = state_ref.shape[0] // 4
    for first, target_ref in ((0, even_ref), (1, odd_ref)):
        paired = (slab ^ 1) < slabs
        if first == 1:
            paired = jnp.logical_and(slab > 0, ((slab - 1) ^ 1) + 1 < slabs)
        top = upward if first == 0 else jnp.logical_not(upward)
        swap = crosses(first, top)

        def fill(ref, target_ref=target_ref, top=top, paired=paired):
            low = ref[pl.ds(0, rows, stride=4), :]
            high = ref[pl.ds(3, rows, stride=4), :]
            target_ref[:rows, :] = jnp.where(paired, jnp.where(top, high, low), 0.0)

        if isinstance(swap, bool):
            fill(swapped_ref if swap else state_ref)
        else:
            pl.when(swap)(lambda fill=fill: fill(swapped_ref))
            pl.when(jnp.logical_not(swap))(lambda fill=fill: fill(state_ref))


def pack_kernel(
    times,
    fields,
    held,
    swapped_ref,
    edge_ref,
    place_ref,
    state_ref,
    x_ref,
    y_ref,
    d_ref,
    even_ref,
    odd_ref,
):
    even = lax.rem(lax.axis_index("sec"), 2) == 0
    for distance, packed_ref in ((1, x_ref), (2, y_ref), (3, d_ref)):
        ahead = jnp.int32(2)
        if distance != 2:
            ahead = jnp.where(even, distance, 4 - distance)
        for j in range(held):
            t = place_ref[(4 + ahead) * times + j]
            for f in range(fields):
                start = (t * fields + f) * 16 + 12
                packed_ref[j * fields + f] = swapped_ref[pl.ds(start, 4), :]
        if distance != 2:
            for a in range(4):
                packed_ref[held * fields + a] = edge_ref[a]
    span_kernel(state_ref, swapped_ref, even_ref, odd_ref)


def inner_kernel(
    times,
    fields,
    state_ref,
    coeff_ref,
    jac_ref,
    omega_ref,
    _,
    partial_ref,
    mix_ref,
):
    lane = lax.broadcasted_iota(jnp.int32, (8, 128), 1)
    sub = lax.broadcasted_iota(jnp.int32, (8, 128), 0)
    lower = sub < 4
    bottom = sub % 4 == 0
    top = sub % 4 == 3
    coeff = [0.1 * coeff_ref[0:8, :], 0.1 * coeff_ref[8:16, :]]
    own = [0.8 - 4.0 * c for c in coeff]
    rate = -0.1 * omega_ref[0]
    weight = [0.0]
    weight += [0.5 * (-1.0) ** m / math.sin(math.pi * m / times) for m in range(1, times)]

    field = (lane // 2) % fields
    sign = jnp.where(lane % 2 == 0, -0.05, 0.05)
    for distance in range(1 - fields, fields):
        mix = jnp.zeros((8, 128), jnp.float32)
        for f in range(max(0, distance), min(fields, fields + distance)):
            mix = jnp.where(field == f, jac_ref[f, 0, f - distance], mix)
        mix_ref[fields - 1 + distance] = sign * mix

    def step(t, _):
        def load(u, f, h):
            start = pl.multiple_of((u * fields + f) * 16 + 8 * h, 8)
            return state_ref[pl.ds(start, 8), :]

        difference, result = [], []
        for f in range(fields):
            v0, v1 = load(t, f, 0), load(t, f, 1)
            r0, r1 = pltpu.roll(v0, 4, 0), pltpu.roll(v1, 4, 0)
            middle = jnp.where(lower, r0, r1)
            axial = [middle + jnp.where(lower, 0.0, r0), jnp.where(lower, r1, 0.0) + middle]
            differences, results = [], []
            for h, v in enumerate((v0, v1)):
                plus = jnp.where(lane == 127, 0.0, pltpu.roll(v, 127, 1))
                minus = jnp.where(lane == 0, 0.0, pltpu.roll(v, 1, 1))
                up = jnp.where(top, 0.0, pltpu.roll(v, 7, 0))
                down = jnp.where(bottom, 0.0, pltpu.roll(v, 1, 0))
                differences.append(plus - minus)
                value = own[h] * v + coeff[h] * ((plus + minus) + (up + down)) + 0.1 * axial[h]
                spectral = jnp.zeros_like(v)
                for m in range(1, times // 2 + 1):
                    before = load(lax.rem(t + times - m, times), f, h)
                    after = load(lax.rem(t + m, times), f, h)
                    spectral = spectral + weight[m] * (before - after)
                results.append(value + rate * spectral)
            difference.append(differences)
            result.append(results)
        for f in range(fields):
            for h in range(2):
                value = result[f][h]
                for g in range(fields):
                    value = value + (-0.05 * jac_ref[f, 0, g]) * difference[g][h]
                start = pl.multiple_of((t * fields + f) * 16 + 8 * h, 8)
                partial_ref[pl.ds(start, 8), :] = value
        return 0

    lax.fori_loop(0, times, step, 0)


def edge_terms(fields, mix_ref, coeff_ref, edge_a_ref, edge_b_ref):
    even = lax.rem(lax.axis_index("sec"), 2) == 0
    sides = lax.broadcasted_iota(jnp.int32, (8, 128), 1) % 2 == 0
    terms = []
    for h in range(2):
        edge_a = jnp.concatenate([edge_a_ref[2 * h], edge_a_ref[2 * h + 1]], axis=0)
        edge_b = jnp.concatenate([edge_b_ref[2 * h], edge_b_ref[2 * h + 1]], axis=0)
        plus_edge = jnp.where(even, edge_a, edge_b)
        minus_edge = jnp.where(even, edge_b, edge_a)
        halo = jnp.where(sides, pltpu.roll(plus_edge, 127, 1), pltpu.roll(minus_edge, 1, 1))
        coeff = 0.1 * coeff_ref[8 * h : 8 * h + 8, :]
        term = jnp.where(sides, coeff[:, 127:128], coeff[:, 0:1]) * halo
        for distance in range(1 - fields, fields):
            term = term + mix_ref[fields - 1 + distance] * pltpu.roll(halo, (2 * distance) % 128, 1)
        terms.append(term)
    return terms


def sector_kernel(
    times, fields, partial_ref, mix_ref, place_ref, coeff_ref, edge_a_ref, edge_b_ref, *rest
):
    source_refs, total_ref = rest[:-1], rest[-1]
    lane = lax.broadcasted_iota(jnp.int32, (8, 128), 1)
    lower = lax.broadcasted_iota(jnp.int32, (8, 128), 0) < 4
    lane4 = lax.broadcasted_iota(jnp.int32, (4, 128), 1)
    outside = jnp.logical_or(lane == 0, lane == 127)
    edges = edge_terms(fields, mix_ref, coeff_ref, edge_a_ref, edge_b_ref)

    def pick(slot, place, t, f):
        if len(source_refs) == 1:
            return source_refs[0][slot, pl.ds((place * fields + f) * 4, 4), :]
        value = source_refs[0][pl.ds((t * fields + f) * 16 + 12, 4), :]
        for other in range(1, 4):
            value = jnp.where(slot == other, source_refs[other][place * fields + f], value)
        return value

    def step(t, _):
        near, near_place, far, far_place, part = [place_ref[5 * t + n] for n in range(5)]
        for f in range(fields):
            index = t * fields + f
            ghost = jnp.where(
                lane4 >= 128 - part, pick(far, far_place, t, f), pick(near, near_place, t, f)
            )
            ghost = pltpu.roll(ghost, jnp.bitwise_and(part, 127), 1)
            ghost = jnp.concatenate([ghost, ghost], axis=0)
            for h in range(2):
                rows = pl.ds(pl.multiple_of(index * 16 + 8 * h, 8), 8)
                value = partial_ref[rows, :]
                value = value + jnp.where(outside, pltpu.roll(edges[h], 127 - 2 * index, 1), 0.0)
                if h == 1:
                    value = value + jnp.where(lower, 0.0, 0.1 * ghost)
                total_ref[rows, :] = value
        return 0

    lax.fori_loop(0, times, step, 0, unroll=9)


def finish_kernel(
    times, fields, total_ref, coeff_ref, even_ref, odd_ref, out_ref, result_ref, sems
):
    straight = lax.rem(lax.axis_index("span"), 2) == 0
    coeff = []
    for s in (0, 3):
        four = 0.1 * coeff_ref[pl.ds(s, 4, stride=4), :]
        coeff.append(jnp.concatenate([four, four], axis=0))

    def piece(n, first, last):
        rows = pl.ds(first * fields * 16, (last - first) * fields * 16)
        return pltpu.make_async_copy(result_ref.at[rows, :], out_ref.at[rows, :], sems.at[n])

    pieces = [(first, min(first + 2, times)) for first in range(0, times, 2)]
    for n, (first, last) in enumerate(pieces):
        low, high = first * fields * 4, last * fields * 4
        for start in range(low, high, 8):
            size = min(8, high - start)
            even, odd = even_ref[start : start + size, :], odd_ref[start : start + size, :]
            halos = jnp.where(straight, odd, even), jnp.where(straight, even, odd)
            for s, halo, factor in zip((0, 3), halos, coeff):
                rows = pl.ds(4 * start + s, size, stride=4)
                result_ref[rows, :] = total_ref[rows, :] + factor[:size] * halo
        piece(n, first, last).start()
    for n, (first, last) in enumerate(pieces):
        piece(n, first, last).wait()


def exchange(times, fields, held, swapped, local, edge, place, coeff, jacobian, frequency):
    f32 = jnp.float32
    tiles, cells = times * fields, local.shape[1]
    sectors, slabs = lax.axis_size("sec"), lax.axis_size("span")
    if held is None:
        even, odd = pl.pallas_call(
            span_kernel,
            out_shape=[pltpu.VMEM((tiles * 4, cells), f32)] * 2,
            in_specs=[VMEM] * 2,
            out_specs=[VMEM] * 2,
            compiler_params=LIMIT,
            name="spans",
        )(local, swapped)
        strip = swapped.reshape(tiles, 16, cells)[:, 12:].reshape(tiles * 4, cells)
        sources = [lax.all_gather(strip, "sec")]
        edge_a = lax.ppermute(edge, "sec", sector_pairs(sectors, 0))
        edge_b = lax.ppermute(edge, "sec", sector_pairs(sectors, 1))
        sent = edge
    else:
        *packed, even, odd = pl.pallas_call(
            lambda *refs: pack_kernel(times, fields, held, *refs),
            out_shape=[
                pltpu.VMEM((held * fields + extra, 4, cells), f32) for extra in (4, 8, 4)
            ]
            + [pltpu.VMEM((tiles * 4 + (32 if held == times else 0), cells), f32)] * 2,
            in_specs=[VMEM, VMEM, SMEM, VMEM],
            out_specs=[VMEM] * 5,
            compiler_params=LIMIT,
            name="pack",
        )(swapped, edge, place, local)
        sent = packed[0]
        near = [
            lax.ppermute(block, "sec", [(k, k ^ distance) for k in range(sectors)])
            for distance, block in zip((1, 2, 3), packed)
        ]
        sources = [swapped] + near
        edge_a, edge_b = near[0][held * fields :], near[2][held * fields :]
    even = lax.ppermute(even, ("row", "span"), slab_pairs(slabs, 0))
    odd = lax.ppermute(odd, ("row", "span"), slab_pairs(slabs, 1))
    partial, mix = pl.pallas_call(
        lambda *refs: inner_kernel(times, fields, *refs),
        out_shape=[
            pltpu.VMEM((tiles * 16, cells), f32),
            pltpu.VMEM((2 * fields - 1, 8, cells), f32),
        ],
        in_specs=[VMEM, VMEM, SMEM, SMEM, ANY],
        out_specs=[VMEM, VMEM],
        compiler_params=LIMIT,
        cost_estimate=pl.CostEstimate(
            flops=tiles * 16 * cells * 50000, bytes_accessed=tiles * 16 * cells * 8000, transcendentals=0
        ),
        name="inner",
    )(local, coeff, jacobian, frequency, sent)
    total = pl.pallas_call(
        lambda *refs: sector_kernel(times, fields, *refs),
        out_shape=pltpu.VMEM((tiles * 16, cells), f32),
        in_specs=[VMEM, VMEM, SMEM] + [VMEM] * (3 + len(sources)),
        out_specs=VMEM,
        compiler_params=LIMIT,
        name="sectors",
    )(partial, mix, place, coeff, edge_a, edge_b, *sources)
    out, _ = pl.pallas_call(
        lambda *refs: finish_kernel(times, fields, *refs),
        out_shape=[pltpu.HBM((tiles * 16, cells), f32), pltpu.VMEM((tiles * 16, cells), f32)],
        in_specs=[VMEM] * 4,
        out_specs=[ANY, VMEM],
        scratch_shapes=[pltpu.SemaphoreType.DMA(((times + 1) // 2,))],
        input_output_aliases={0: 1},
        compiler_params=LIMIT,
        name="finish",
    )(total, coeff, even, odd)
    return out


def on_device(state, viscosity, jacobian, frequency, offsets):
    _, times, fields, axial, spans, cells = state.shape
    tiles = times * fields
    sectors, slabs = lax.axis_size("sec"), lax.axis_size("span")
    flat = state.reshape(tiles * 16, cells)
    coeff = viscosity.reshape(16, cells)
    f32 = jnp.float32
    swapped = lax.ppermute(flat, "row", [(0, 1), (1, 0)])
    local, edge, coeff, jac, place, size = pl.pallas_call(
        lambda *refs: collect_kernel(times, fields, *refs),
        out_shape=[
            pltpu.VMEM((tiles * 16, cells), f32),
            pltpu.VMEM((4, 4, cells), f32),
            pltpu.VMEM((16, cells), f32),
            pltpu.SMEM((fields, 1, fields), f32),
            pltpu.SMEM((8 * times,), jnp.int32),
            pltpu.SMEM((1,), jnp.int32),
        ],
        in_specs=[ANY] * 4,
        out_specs=[VMEM] * 3 + [SMEM] * 3,
        scratch_shapes=[
            pltpu.SMEM((times,), jnp.int32),
            pltpu.SemaphoreType.DMA((times,)),
            pltpu.SemaphoreType.DMA((3,)),
        ],
        compiler_params=LIMIT,
        name="collect",
    )(
        *(
            pltpu.with_memory_space_constraint(x, pltpu.HBM)
            for x in (flat, coeff, jnp.swapaxes(jacobian, 0, 1), offsets)
        )
    )
    operands = (swapped, local, edge, place, coeff, jac, frequency)
    if sectors == 4:
        branches = [
            lambda *held_operands, held=held: exchange(times, fields, held, *held_operands)
            for held in range((times + 1) // 2, times + 1)
        ]
        out = lax.switch(size[0], branches, *operands)
    else:
        out = exchange(times, fields, None, *operands)
    return out.reshape(state.shape)


def solution(mesh):
    return jax.shard_map(
        on_device,
        mesh=mesh,
        in_specs=(
            P("row", None, None, None, "span", "sec"),
            P("row", None, "span", "sec"),
            P("row", None, None),
            P("row"),
            P(),
        ),
        out_specs=P("row", None, None, None, "span", "sec"),
        check_vma=False,
    )
```
